256 devices in a mesh: chan: 16 (over z_lo, x, core), space: 16 (over y, z_hi).
Axes of the slice: x: 4, y: 4, z: 8 (z_hi: 4, z_lo: 2; z = z_hi * 2 + z_lo), core: 2. Of those that a mesh axis runs over, the one named last changes fastest.
Arguments:
- upsampled: bfloat16 [256, 1, 256, 256], P('chan', None, 'space'), may hold values from -6 to 6
- skip_features: bfloat16 [256, 1, 256, 256], P('chan', None, 'space'), may hold values from -6 to 6
- conv_weight: bfloat16 [256, 9, 512], P('chan'), may hold values from -0.09375 to 0.09375
- grad_output: bfloat16 [256, 1, 256, 256], P('chan', None, 'space'), may hold values from -6 to 6
Outputs:
- activation: bfloat16 [256, 1, 256, 256], P('chan', None, 'space')
- grad_upsampled: bfloat16 [256, 1, 256, 256], P('chan', None, 'space')
- grad_skip: bfloat16 [256, 1, 256, 256], P('chan', None, 'space')
- weight_grad: float32 [256, 9, 512], P('chan', None, 'space')
The draws below stay inside these ranges and needn't reach their ends.
All inputs are finite; a program needn't handle non-finite values.
Results may differ from the reference program's by a relative error of at most 0.018.
Values may be sent and summed in bfloat16 or wider, within the bound.
No kernel may reach another device: no remote copies, remote signals or barrier semaphores. Data moves between devices by JAX's collectives and lax.ppermute only.
A program may use at most 128 MiB of HBM per device.

```python
import jax
import jax.numpy as jnp
from jax import lax

CU = 256
CS = 256
CO = 256
B = 1
W = 256
H = 256
CI = 512


def shard_levels(stream_key, extent, split, low, largest):
    level = 1.0
    for dim, parts in split:
        steps = jax.random.uniform(jax.random.fold_in(jax.random.fold_in(stream_key, 6), dim), (parts,), jnp.float32, low / len(split), largest / len(split))
        level = level * jnp.repeat(jnp.exp(steps), extent[dim] // parts).reshape((-1,) + (1,) * (len(extent) - 1 - dim))
    return level


def gaussian(rng, extent, scale, most, shards=(), held_as=jnp.bfloat16):
    values = scale * jax.random.normal(rng, extent, jnp.float32)
    if shards:
        values = values * shard_levels(rng, extent, shards, -0.22, 0.18)
    return jnp.clip(values, -most, most).astype(held_as)


def setup_inputs(seed: int = 0) -> dict:
    keys = jax.random.split(jax.random.key(seed), 5)
    return {
        "upsampled": gaussian(keys[0], (CU, B, H, W), 1.0, 6.0, ((0, 16), (2, 16))),
        "skip_features": gaussian(keys[1], (CS, B, H, W), 1.0, 6.0, ((0, 16), (2, 16))),
        "conv_weight": gaussian(keys[2], (CO, 9, CI), (9 * CI) ** -0.5, 0.09375, ((0, 16),)),
        "grad_output": gaussian(keys[3], (CO, B, H, W), 1.0, 6.0, ((0, 16), (2, 16))),
    }


def convolve(field, kernel):
    return lax.conv_general_dilated(field, kernel, (1, 1), ((1, 1), (1, 1)), dimension_numbers=('CNHW', 'OHWI', 'CNHW'), preferred_element_type=jnp.float32)

def reference(upsampled, skip_features, conv_weight, grad_output):
    features = jnp.concatenate([upsampled, skip_features], 0)
    channels = features.shape[0]
    filters = conv_weight.shape[0]
    height = features.shape[2]
    width = features.shape[3]
    kernel = conv_weight.reshape(filters, 3, 3, channels)
    preact = convolve(features, kernel)
    sigmoid_val = jax.nn.sigmoid(preact)
    activation = (preact * sigmoid_val).astype(jnp.bfloat16)
    grad_pre = (grad_output.astype(jnp.float32) * sigmoid_val * (1.0 + preact * (1.0 - sigmoid_val))).astype(jnp.bfloat16)
    flipped = jnp.flip(kernel, (1, 2)).transpose(3, 1, 2, 0)
    grad_features = convolve(grad_pre, flipped).astype(jnp.bfloat16)
    padded = jnp.pad(features, ((0, 0), (0, 0), (1, 1), (1, 1)))
    flat_grad = grad_pre.reshape(filters, -1)
    terms = []
    for row_off in range(3):
        for col_off in range(3):
            window = padded[:, :, row_off:row_off + height, col_off:col_off + width].reshape(channels, -1)
            terms.append(jnp.dot(flat_grad, window.T, preferred_element_type=jnp.float32))
    count = grad_pre.shape[1] * height * width
    weight_grad = jnp.stack(terms, 1) / jnp.sqrt(jnp.float32(count))
    half = upsampled.shape[0]
    return (activation, grad_features[:half], grad_features[half:], weight_grad)
```

```python
import functools
import math

import jax
import jax.numpy as jnp
from jax import lax
from jax.experimental import pallas as pl
from jax.experimental.pallas import tpu as pltpu
from jax.sharding import PartitionSpec as P

NZ, NX, NC = 2, 4, 2
PEERS = NZ * NX * NC
NY, NH = 4, 4
W = 256
OWN = 16
HALF = OWN // NZ
ROWS = OWN // NX
FILT = PEERS * HALF
CHAN = PEERS * OWN
TAPS = 9

FEAT = (ROWS + 2) * OWN
GOUT = ROWS * HALF
WTAP = TAPS * HALF
WPAD = 80
IN_BLOCK = FEAT + GOUT + WPAD
GRAD = ROWS * OWN
ACT = (ROWS // NC) * HALF
OUT_BLOCK = GRAD + ACT + WPAD

bf16 = jnp.bfloat16
f32 = jnp.float32


def call(body, outs, scratch=(), flops=0, nbytes=0, vmem=32):
    return pl.pallas_call(
        body,
        out_shape=[jax.ShapeDtypeStruct(s, t) for s, t in outs],
        scratch_shapes=[pltpu.VMEM(s, t) for s, t in scratch],
        compiler_params=pltpu.CompilerParams(vmem_limit_bytes=vmem * 1024 * 1024),
        cost_estimate=pl.CostEstimate(
            flops=flops, bytes_accessed=nbytes, transcendentals=0
        ),
    )


def picks(rows, cols, source):
    d = lax.broadcasted_iota(jnp.int32, (rows, cols), 0)
    s = lax.broadcasted_iota(jnp.int32, (rows, cols), 1)
    return jnp.where(source(d) == s, 1.0, 0.0).astype(bf16)


def move(matrix, x):
    return jnp.dot(matrix, x, preferred_element_type=f32).astype(bf16)


def swapped(d):
    return ((d & 15) << 4) | (d >> 4)


def gout_source(d):
    f8, row, x, z = d & 7, (d >> 3) & 3, (d >> 5) & 3, d >> 7
    return (z << 7) | (f8 << 4) | (x << 2) | row


def w_source(d):
    z = (d >= WPAD).astype(jnp.int32)
    e = d - z * WPAD
    return jnp.where(e < WTAP, ((e >> 3) << 4) + z * HALF + (e & 7), -1)


def act_source(d):
    f, r = d >> 4, d & 15
    return ((f >> 3) << 7) | (r << 3) | (f & 7)


def pack(up, skip, gout, w, before, after, out):
    swap = picks(OWN * OWN, OWN * OWN, swapped)
    rows = []
    for c, ref in enumerate((up, skip)):
        own = move(swap, ref[...])
        edge = slice(c * OWN, (c + 1) * OWN)
        rows.append(jnp.concatenate([before[edge, :], own, after[edge, :]], 0))
    g = move(picks(OWN * OWN, OWN * OWN, gout_source), gout[...])
    wt = move(picks(NZ * WPAD, TAPS * OWN, w_source), w[...])
    for z in range(NZ):
        for x in range(NX):
            for c in range(NC):
                t = (z * NX + x) * NC + c
                out[t, 0:FEAT, :] = rows[c][x * ROWS * OWN : x * ROWS * OWN + FEAT, :]
                part = (z * NX + x) * GOUT
                out[t, FEAT : FEAT + GOUT, :] = g[part : part + GOUT, :]
                out[t, FEAT + GOUT :, :] = wt[
                    z * WPAD : (z + 1) * WPAD, c * W : (c + 1) * W
                ]


def column(n=W):
    return lax.broadcasted_iota(jnp.int32, (1, n), 1)


def from_left(x):
    return jnp.where(column() == 0, 0.0, pltpu.roll(x, 1, 1))


def from_right(x):
    return jnp.where(column() == W - 1, 0.0, pltpu.roll(x, W - 1, 1))


def forward(block, part, gout, feat, wback, wfwd):
    for r in range(ROWS + 2):
        for s in range(PEERS):
            at = r * CHAN + s * OWN
            feat[at : at + OWN, :] = block[s, r * OWN : (r + 1) * OWN, :]
    wt = block[:, FEAT + GOUT :, :].astype(f32)
    for p in range(3):
        for q in range(3):
            tap = 3 * p + q
            piece = wt[:, tap * HALF : (tap + 1) * HALF, :].reshape(FILT, W).astype(bf16)
            wfwd[q * FILT : (q + 1) * FILT, p * W : (p + 1) * W] = piece
            wback[(2 - p) * FILT : (3 - p) * FILT, q * W : (q + 1) * W] = piece
    g = block[:, FEAT : FEAT + GOUT, :].astype(f32)
    for r in range(ROWS):
        piece = g[:, r * HALF : (r + 1) * HALF, :].reshape(FILT, W)
        gout[r * FILT : (r + 1) * FILT, :] = piece.astype(bf16)
        y = jnp.dot(
            wfwd[...], feat[r * CHAN : (r + 3) * CHAN, :], preferred_element_type=f32
        )
        part[r * FILT : (r + 1) * FILT, :] = (
            from_left(y[:FILT]) + y[FILT : 2 * FILT] + from_right(y[2 * FILT :])
        )


def gate(mine, other, gout, act, grad, first, last, rows):
    core = lax.rem(lax.axis_index("chan"), NC)
    for r in range(ROWS):
        at = slice(r * FILT, (r + 1) * FILT)
        pre = mine[at, :] + other[at, :]
        s = jax.nn.sigmoid(pre)
        rows[at, :] = pre * s
        g = (gout[at, :].astype(f32) * s * (1.0 + pre * (1.0 - s))).astype(bf16)
        grad[at, :] = g
        if r == 0:
            first[...] = g
        if r == ROWS - 1:
            last[...] = g
    n = ROWS // NC
    kept = rows[pl.ds(pl.multiple_of(core * n * FILT, FILT), n * FILT), :]
    kept = kept.reshape(n, PEERS, HALF, W)
    kept = jnp.concatenate([kept[i] for i in range(n)], axis=1)
    act[...] = kept.astype(bf16)


def weight_part(grad, feat, out, acc):
    g = grad[...].astype(f32)
    sides = []
    for moved in (from_right(g), g, from_left(g)):
        m = moved.astype(bf16)
        sides.append(
            jnp.concatenate([m[r * FILT : (r + 1) * FILT] for r in range(ROWS)], 1)
        )
    sides = jnp.concatenate(sides, 0)
    acc[:, WTAP:, :] = jnp.zeros((PEERS, WPAD - WTAP, W), f32)
    for p in range(3):
        f = jnp.concatenate(
            [feat[(r + p) * CHAN : (r + p + 1) * CHAN, :] for r in range(ROWS)], 1
        )
        d = lax.dot_general(
            sides, f, (((1,), (1,)), ((), ())), preferred_element_type=f32
        )
        for q in range(3):
            tap = 3 * p + q
            acc[:, tap * HALF : (tap + 1) * HALF, :] = d[
                q * FILT : (q + 1) * FILT
            ].reshape(PEERS, HALF, W)
    out[...] = acc[...].astype(bf16)


def backward(grad, before, after, wback, wpart, act, out, rows):
    rows[0:FILT, :] = before[...]
    rows[FILT : (ROWS + 1) * FILT, :] = grad[...]
    rows[(ROWS + 1) * FILT :, :] = after[...]
    for r in range(ROWS):
        y = lax.dot_general(
            wback[...],
            rows[r * FILT : (r + 3) * FILT, :],
            (((0,), (0,)), ((), ())),
            preferred_element_type=f32,
        )
        g = from_right(y[:CHAN]) + y[CHAN : 2 * CHAN] + from_left(y[2 * CHAN :])
        out[:, r * OWN : (r + 1) * OWN, :] = g.astype(bf16).reshape(PEERS, OWN, W)
    out[:, GRAD : GRAD + ACT, :] = act[...]
    out[:, GRAD + ACT :, :] = wpart[...]


def weight_pieces(block, own, one, two, three, pieces):
    y = lax.div(lax.axis_index("space"), NH)
    halves = []
    for c in range(NC):
        parts = []
        for z in range(NZ):
            total = 0.0
            for x in range(NX):
                t = (z * NX + x) * NC + c
                total = total + block[t, GRAD + ACT :, :].astype(f32)
            parts.append(total[:WTAP].reshape(TAPS, HALF, W))
        halves.append(jnp.concatenate(parts, 1).reshape(TAPS * OWN, W))
    for k in range(NY):
        pieces[k] = halves[k // 2][:, (k % 2) * 128 : (k % 2) * 128 + 128]
    own[...] = pieces[y]
    for k, ref in enumerate((one, two, three)):
        ref[...] = pieces[lax.rem(y + k + 1, NY)].astype(bf16)


def unpack(block, act, grad_up, grad_skip):
    swap = picks(OWN * OWN, OWN * OWN, swapped)
    for c, ref in enumerate((grad_up, grad_skip)):
        rows = []
        for x in range(NX):
            t = x * NC + c
            rows.append(
                block[t, :GRAD, :].astype(f32)
                + block[t + NX * NC, :GRAD, :].astype(f32)
            )
        ref[...] = move(swap, jnp.concatenate(rows, 0).astype(bf16))
    a = block[:, GRAD : GRAD + ACT, :].reshape(PEERS * ACT, W)
    act[...] = move(picks(OWN * OWN, OWN * OWN, act_source), a)


def add_pieces(own, one, two, three, total, sent):
    t = own[...] + one[...].astype(f32) + two[...].astype(f32) + three[...].astype(f32)
    total[...] = t
    sent[...] = t.astype(bf16)


def finish(factor, own, one, two, three, out):
    h = lax.rem(lax.axis_index("space"), NH)
    t = own[...] + one[...].astype(f32) + two[...].astype(f32) + three[...].astype(f32)
    t = pltpu.roll(t, lax.rem(128 - h * 32, 128), 1)
    out[...] = t[:, :32] * factor


def shards(upsampled, skip_features, conv_weight, grad_output):
    tiles = lax.axis_size("space")
    width = grad_output.shape[3]
    factor = 1.0 / math.sqrt(grad_output.shape[1] * grad_output.shape[2] * tiles * width)

    down = [(i, i + 1) for i in range(tiles - 1)]
    up = [(j, i) for i, j in down]

    def edge(r):
        return jnp.concatenate([upsampled[:, 0, r, :], skip_features[:, 0, r, :]], 0)

    before = lax.ppermute(edge(OWN - 1), "space", down)
    after = lax.ppermute(edge(0), "space", up)
    n = OWN * OWN
    (sent,) = call(pack, [((PEERS, IN_BLOCK, W), bf16)])(
        upsampled.reshape(n, W),
        skip_features.reshape(n, W),
        grad_output.reshape(n, W),
        conv_weight.transpose(1, 0, 2).reshape(TAPS * OWN, 2 * W),
        before,
        after,
    )
    block = lax.all_to_all(sent, "chan", 0, 0, tiled=True)
    part, gout, feat, wback = call(
        forward,
        [
            ((ROWS * FILT, W), f32),
            ((ROWS * FILT, W), bf16),
            (((ROWS + 2) * CHAN, W), bf16),
            ((3 * FILT, 3 * W), bf16),
        ],
        [((3 * FILT, 3 * W), bf16)],
    )(block)
    other = lax.ppermute(part, "chan", [(i, i ^ 1) for i in range(PEERS)])
    act, grad, first, last = call(
        gate,
        [
            ((PEERS, ACT, W), bf16),
            ((ROWS * FILT, W), bf16),
            ((FILT, W), bf16),
            ((FILT, W), bf16),
        ],
        [((ROWS * FILT, W), f32)],
    )(part, other, gout)

    def place(z, x, c, s):
        return ((z * NX + x) * NC + c) * tiles + s

    nxt = []
    for z in range(NZ):
        for c in range(NC):
            line = [place(z, x, c, s) for s in range(tiles) for x in range(NX)]
            nxt += list(zip(line[:-1], line[1:]))
    g_before = lax.ppermute(last, ("chan", "space"), nxt)
    g_after = lax.ppermute(first, ("chan", "space"), [(j, i) for i, j in nxt])
    (wpart,) = call(
        weight_part, [((PEERS, WPAD, W), bf16)], [((PEERS, WPAD, W), f32)]
    )(grad, feat)
    (sent,) = call(
        backward,
        [((PEERS, OUT_BLOCK, W), bf16)],
        [(((ROWS + 2) * FILT, W), bf16)],
    )(grad, g_before, g_after, wback, wpart, act)
    block = lax.all_to_all(sent, "chan", 0, 0, tiled=True)

    piece = (TAPS * OWN, 128)
    pieces = call(
        weight_pieces,
        [(piece, f32)] + [(piece, bf16)] * 3,
        [((NY,) + piece, f32)],
    )(block)
    got = [
        lax.ppermute(
            pieces[k],
            "space",
            [
                (y * NH + h, ((y + k) % NY) * NH + h)
                for y in range(NY)
                for h in range(NH)
            ],
        )
        for k in range(1, NY)
    ]
    activation, grad_up, grad_skip = call(unpack, [((n, W), bf16)] * 3)(block)
    total, half = call(add_pieces, [(piece, f32), (piece, bf16)])(pieces[0], *got)
    got = [
        lax.ppermute(
            half,
            "space",
            [
                (y * NH + h, y * NH + (h + k) % NH)
                for y in range(NY)
                for h in range(NH)
            ],
        )
        for k in range(1, NH)
    ]
    (wgrad,) = call(functools.partial(finish, factor), [((TAPS * OWN, 32), f32)])(
        total, *got
    )
    shape = upsampled.shape
    return (
        activation.reshape(shape),
        grad_up.reshape(shape),
        grad_skip.reshape(shape),
        wgrad.reshape(TAPS, OWN, 32).transpose(1, 0, 2),
    )


def solution(mesh):
    tile = P("chan", None, "space", None)
    in_specs = (tile, tile, P("chan", None, None), tile)
    out_specs = (tile, tile, tile, P("chan", None, "space"))
    return jax.shard_map(
        shards, mesh=mesh, in_specs=in_specs, out_specs=out_specs, check_vma=False
    )
```

```python
import functools
import math

import jax
import jax.numpy as jnp
from jax import lax
from jax.experimental import pallas as pl
from jax.experimental.pallas import tpu as pltpu
from jax.sharding import PartitionSpec as P

NZ, NX, NC = 2, 4, 2
PEERS = NZ * NX * NC
NY, NH = 4, 4
W = 256
OWN = 16
HALF = OWN // NZ
ROWS = OWN // NX
FILT = PEERS * HALF
CHAN = PEERS * OWN
TAPS = 9

FROWS = ROWS + 4
GROWS = ROWS + 2
FEAT = FROWS * OWN
GHALF = GROWS // NC
GOUT = GHALF * HALF
IN_BLOCK = FEAT + GOUT + TAPS * HALF
EDGE = 2 * 2 * OWN + OWN
GRAD = ROWS * OWN
ACT = (ROWS // NC) * HALF
OUT_BLOCK = GRAD + ACT + TAPS * HALF
GROUPS = TAPS * OWN // 8
PIECE = -(-GROUPS // 4) * 8

bf16 = jnp.bfloat16
f32 = jnp.float32


def call(body, outs, scratch=(), in_specs=None, vmem=32):
    specs = {} if in_specs is None else {"in_specs": in_specs}
    return pl.pallas_call(
        body,
        out_shape=[jax.ShapeDtypeStruct(s, t) for s, t in outs],
        scratch_shapes=[pltpu.VMEM(*s) if isinstance(s, tuple) else s for s in scratch],
        compiler_params=pltpu.CompilerParams(vmem_limit_bytes=vmem * 1024 * 1024),
        **specs,
    )


def picks(rows, cols, source):
    d = lax.broadcasted_iota(jnp.int32, (rows, cols), 0)
    s = lax.broadcasted_iota(jnp.int32, (rows, cols), 1)
    return jnp.where(source(d) == s, 1.0, 0.0).astype(bf16)


def move(matrix, x):
    return jnp.dot(matrix, x, preferred_element_type=f32).astype(bf16)


def swapped(d):
    return ((d & 15) << 4) | (d >> 4)


def gout_source(d):
    f8, core, x, z, i = d & 7, (d >> 3) & 1, (d >> 4) & 3, (d >> 6) & 1, d >> 7
    r = (x << 2) - 1 + core * GHALF + i
    f = (z << 3) | f8
    inside = (f << 4) + r
    return jnp.where(r < 0, 256 + f, jnp.where(r > 15, 272 + f, inside))


def act_source(d):
    f, r = d >> 4, d & 15
    return ((f >> 3) << 7) | (r << 3) | (f & 7)


def fetch(srcs, dsts, sems):
    copies = [
        pltpu.make_async_copy(src, dst, sems.at[i])
        for i, (src, dst) in enumerate(zip(srcs, dsts))
    ]
    for copy in copies:
        copy.start()
    return copies


def edges(up, skip, gout, down, above, u, k, g, sems):
    copies = fetch((up, skip, gout), (u, k, g), sems)
    n = 2 * OWN
    top = picks(n, OWN * OWN, swapped)
    bottom = picks(n, OWN * OWN, lambda d: swapped(d + OWN * OWN - n))
    for i, ref in enumerate((u, k)):
        copies[i].wait()
        x = ref[...]
        above[i * n : (i + 1) * n, :] = move(top, x)
        down[i * n : (i + 1) * n, :] = move(bottom, x)
    copies[2].wait()
    x = g[...]
    above[2 * n :, :] = move(top[:OWN], x)
    down[2 * n :, :] = move(bottom[OWN:], x)


def by_row(up, skip, gout, w, up_rows, skip_rows, g_out, w_out):
    swap = picks(OWN * OWN, OWN * OWN, swapped)
    up_rows[...] = move(swap, up[...])
    skip_rows[...] = move(swap, skip[...])
    g_out[...] = gout[...]
    w_out[...] = w[...]


def pack(up_rows, skip_rows, gout, w, before, after, out):
    n = 2 * OWN
    s = lax.axis_index("space")
    before = jnp.where(s > 0, before[...].astype(f32), 0.0).astype(bf16)
    after = jnp.where(s < NY * NH - 1, after[...].astype(f32), 0.0).astype(bf16)
    rows = [
        jnp.concatenate(
            [before[i * n : (i + 1) * n, :], ref[...], after[i * n : (i + 1) * n, :]], 0
        )
        for i, ref in enumerate((up_rows, skip_rows))
    ]
    g = jnp.concatenate([gout[...], before[2 * n :, :], after[2 * n :, :]], 0)
    g = jnp.dot(
        picks(GHALF * PEERS * HALF, OWN * OWN + 2 * OWN, gout_source),
        g,
        preferred_element_type=f32,
    )
    wt = w[...].astype(f32)
    for z in range(NZ):
        for x in range(NX):
            for c in range(NC):
                t = (z * NX + x) * NC + c
                out[t, 0:FEAT, :] = rows[c][x * ROWS * OWN : x * ROWS * OWN + FEAT, :]
                parts = [
                    g[(i * PEERS + t) * HALF : (i * PEERS + t + 1) * HALF]
                    for i in range(GHALF)
                ] + [
                    wt[
                        k * OWN + z * HALF : k * OWN + (z + 1) * HALF,
                        c * W : (c + 1) * W,
                    ]
                    for k in range(TAPS)
                ]
                out[t, FEAT:, :] = jnp.concatenate(parts, 0).astype(bf16)


def column(n=W):
    return lax.broadcasted_iota(jnp.int32, (1, n), 1)


def from_left(x):
    return jnp.where(column() == 0, 0.0, pltpu.roll(x, 1, 1))


def from_right(x):
    return jnp.where(column() == W - 1, 0.0, pltpu.roll(x, W - 1, 1))


def forward(block, part, gout, feat, wback, wfwd):
    for r in range(FROWS):
        for s in range(PEERS):
            at = r * CHAN + s * OWN
            feat[at : at + OWN, :] = block[s, r * OWN : (r + 1) * OWN, :]
    rest = block[:, FEAT:, :].astype(f32)
    for i in range(GHALF):
        piece = rest[:, i * HALF : (i + 1) * HALF, :].reshape(FILT, W)
        gout[i * FILT : (i + 1) * FILT, :] = piece.astype(bf16)
    for p in range(3):
        for q in range(3):
            at = GOUT + (3 * p + q) * HALF
            piece = rest[:, at : at + HALF, :].reshape(FILT, W).astype(bf16)
            wfwd[q * FILT : (q + 1) * FILT, p * W : (p + 1) * W] = piece
            wback[(2 - p) * FILT : (3 - p) * FILT, q * W : (q + 1) * W] = piece
    for r in range(GROWS):
        y = jnp.dot(
            wfwd[...], feat[r * CHAN : (r + 3) * CHAN, :], preferred_element_type=f32
        )
        part[r * FILT : (r + 1) * FILT, :] = (
            from_left(y[:FILT]) + y[FILT : 2 * FILT] + from_right(y[2 * FILT :])
        )


def backward(mine, other, g_mine, g_other, feat, wback, out, gout, grad, rows, acc):
    core = lax.rem(lax.axis_index("chan"), NC)
    n = GHALF * FILT
    gout[pl.ds(pl.multiple_of(core * n, FILT), n), :] = g_mine[...]
    gout[pl.ds(pl.multiple_of((1 - core) * n, FILT), n), :] = g_other[...]
    for r in range(GROWS):
        at = slice(r * FILT, (r + 1) * FILT)
        pre = mine[at, :] + other[at, :]
        s = jax.nn.sigmoid(pre)
        rows[at, :] = pre * s
        g = gout[at, :].astype(f32) * s * (1.0 + pre * (1.0 - s))
        grad[at, :] = g.astype(bf16)
    n = ROWS // NC
    kept = rows[pl.ds(pl.multiple_of((1 + core * n) * FILT, FILT), n * FILT), :]
    kept = kept.reshape(n, PEERS, HALF, W)
    for i in range(n):
        acc[:, i * HALF : (i + 1) * HALF, :] = kept[i]

    for r in range(ROWS):
        y = lax.dot_general(
            wback[...],
            grad[r * FILT : (r + 3) * FILT, :],
            (((0,), (0,)), ((), ())),
            preferred_element_type=f32,
        )
        g = from_right(y[:CHAN]) + y[CHAN : 2 * CHAN] + from_left(y[2 * CHAN :])
        out[:, r * OWN : (r + 1) * OWN, :] = g.astype(bf16).reshape(PEERS, OWN, W)

    g = grad[FILT : (ROWS + 1) * FILT, :].astype(f32)
    sides = []
    for moved in (from_right(g), g, from_left(g)):
        m = moved.astype(bf16)
        sides.append(
            jnp.concatenate([m[r * FILT : (r + 1) * FILT] for r in range(ROWS)], 1)
        )
    sides = jnp.concatenate(sides, 0)
    for p in range(3):
        f = jnp.concatenate(
            [feat[(r + p + 1) * CHAN : (r + p + 2) * CHAN, :] for r in range(ROWS)], 1
        )
        d = lax.dot_general(
            sides, f, (((1,), (1,)), ((), ())), preferred_element_type=f32
        )
        for q in range(3):
            at = ACT + (3 * p + q) * HALF
            acc[:, at : at + HALF, :] = d[q * FILT : (q + 1) * FILT].reshape(
                PEERS, HALF, W
            )
    out[:, GRAD:, :] = acc[...].astype(bf16)


def weight_pieces(block, out):
    lane = lax.broadcasted_iota(jnp.int32, (1, 128), 1)
    spaces = NY * NH
    turned = []
    for c in range(NC):
        totals = []
        for z in range(NZ):
            total = 0.0
            for x in range(NX):
                t = (z * NX + x) * NC + c
                total = total + block[t, GRAD:, :].astype(f32)[ACT:]
            totals.append(total)
        for half in range(2):
            at = slice(half * 128, (half + 1) * 128)
            turned.append(
                [
                    [t[:, at] if k == 0 else pltpu.roll(t[:, at], 32 * k, 1) for k in range(4)]
                    for t in totals
                ]
            )
    for s in range(spaces):
        rows = []
        for i in range(PIECE // 8):
            row = jnp.zeros((8, 128), f32)
            for g in range(4):
                tap, z = divmod(4 * i + g, 2)
                if tap < TAPS:
                    part = turned[s // 4][z][(g - s) % 4][tap * 8 : tap * 8 + 8]
                    row = jnp.where(lane // 32 == g, part, row)
            rows.append(row)
        out[s] = jnp.concatenate(rows, 0).astype(bf16)


def unpack(block, act, grad_up, grad_skip):
    swap = picks(OWN * OWN, OWN * OWN, swapped)
    for c, ref in enumerate((grad_up, grad_skip)):
        rows = []
        for x in range(NX):
            t = x * NC + c
            rows.append(
                block[t, :GRAD, :].astype(f32)
                + block[t + NX * NC, :GRAD, :].astype(f32)
            )
        ref[...] = move(swap, jnp.concatenate(rows, 0).astype(bf16))
    a = block[:, GRAD : GRAD + ACT, :].reshape(PEERS * ACT, W)
    act[...] = move(picks(OWN * OWN, OWN * OWN, act_source), a)


def finish(factor, pieces, out):
    t = pieces[0].astype(f32)
    for s in range(1, NY * NH):
        t = t + pieces[s].astype(f32)
    t = t * factor
    for g in range(4):
        part = (t if g == 0 else pltpu.roll(t, 128 - 32 * g, 1))[:, :32]
        for i in range(PIECE // 8):
            k = 4 * i + g
            if k < GROUPS:
                out[k * 8 : k * 8 + 8, :] = part[i * 8 : i * 8 + 8]


def shards(upsampled, skip_features, conv_weight, grad_output):
    tiles = lax.axis_size("space")
    width = grad_output.shape[3]
    factor = 1.0 / math.sqrt(grad_output.shape[1] * grad_output.shape[2] * tiles * width)

    down = [(i, (i + 1) % tiles) for i in range(tiles)]
    up = [(j, i) for i, j in down]

    n = OWN * OWN
    anywhere = pl.BlockSpec(memory_space=pltpu.HBM)
    raw = (
        upsampled.reshape(n, W),
        skip_features.reshape(n, W),
        grad_output.reshape(n, W),
    )
    first, last = call(
        edges,
        [((EDGE, W), bf16)] * 2,
        [((n, W), bf16)] * 3 + [pltpu.SemaphoreType.DMA((3,))],
        in_specs=[anywhere] * 3,
        vmem=56,
    )(*raw)
    before = lax.ppermute(first, "space", down)
    after = lax.ppermute(last, "space", up)
    filters = conv_weight.transpose(1, 0, 2).reshape(TAPS * OWN, 2 * W)
    held = call(by_row, [((n, W), bf16)] * 3 + [((TAPS * OWN, 2 * W), bf16)])(
        *raw, filters
    )
    (sent,) = call(pack, [((PEERS, IN_BLOCK, W), bf16)])(*held, before, after)
    block = lax.all_to_all(sent, "chan", 0, 0, tiled=True)
    part, gout, feat, wback = call(
        forward,
        [
            ((GROWS * FILT, W), f32),
            ((GHALF * FILT, W), bf16),
            ((FROWS * CHAN, W), bf16),
            ((3 * FILT, 3 * W), bf16),
        ],
        [((3 * FILT, 3 * W), bf16)],
    )(block)
    pair = [(i, i ^ 1) for i in range(PEERS)]
    (sent,) = call(
        backward,
        [((PEERS, OUT_BLOCK, W), bf16)],
        [
            ((GROWS * FILT, W), bf16),
            ((GROWS * FILT, W), bf16),
            ((GROWS * FILT, W), f32),
            ((PEERS, OUT_BLOCK - GRAD, W), f32),
        ],
    )(
        part,
        lax.ppermute(part, "chan", pair),
        gout,
        lax.ppermute(gout, "chan", pair),
        feat,
        wback,
    )
    block = lax.all_to_all(sent, "chan", 0, 0, tiled=True)

    (pieces,) = call(weight_pieces, [((tiles, PIECE, 128), bf16)])(block)
    pieces = lax.all_to_all(pieces, "space", 0, 0, tiled=True)
    activation, grad_up, grad_skip = call(unpack, [((n, W), bf16)] * 3)(block)
    (wgrad,) = call(functools.partial(finish, factor), [((TAPS * OWN, 32), f32)])(pieces)
    shape = upsampled.shape
    return (
        activation.reshape(shape),
        grad_up.reshape(shape),
        grad_skip.reshape(shape),
        wgrad.reshape(TAPS, OWN, 32).transpose(1, 0, 2),
    )


def solution(mesh):
    tile = P("chan", None, "space", None)
    in_specs = (tile, tile, P("chan", None, None), tile)
    out_specs = (tile, tile, tile, P("chan", None, "space"))
    return jax.shard_map(
        shards, mesh=mesh, in_specs=in_specs, out_specs=out_specs, check_vma=False
    )
```

```python
import functools
import math

import jax
import jax.numpy as jnp
from jax import lax
from jax.experimental import pallas as pl
from jax.experimental.pallas import tpu as pltpu
from jax.sharding import PartitionSpec as P

NZ, NX, NC = 2, 4, 2
PEERS = NZ * NX * NC
NY, NH = 4, 4
W = 256
OWN = 16
HALF = OWN // NZ
ROWS = OWN // NX
FILT = PEERS * HALF
CHAN = PEERS * OWN
TAPS = 9

FROWS = ROWS + 4
GROWS = ROWS + 2
FEAT = FROWS * OWN
GHALF = GROWS // NC
GOUT = GHALF * HALF
IN_BLOCK = FEAT + GOUT + TAPS * HALF
EDGE = 2 * 2 * OWN + OWN
GRAD = ROWS * OWN
ACT = (ROWS // NC) * HALF
OUT_BLOCK = GRAD + ACT + TAPS * HALF
GROUPS = TAPS * OWN // 8
PIECE = -(-GROUPS // 4) * 8

bf16 = jnp.bfloat16
f32 = jnp.float32


def call(body, outs, scratch=(), in_specs=None, vmem=32):
    specs = {} if in_specs is None else {"in_specs": in_specs}
    return pl.pallas_call(
        body,
        out_shape=[jax.ShapeDtypeStruct(*s) if isinstance(s, tuple) else s for s in outs],
        scratch_shapes=[pltpu.VMEM(*s) if isinstance(s, tuple) else s for s in scratch],
        compiler_params=pltpu.CompilerParams(vmem_limit_bytes=vmem * 1024 * 1024),
        **specs,
    )


def picks(rows, cols, source):
    d = lax.broadcasted_iota(jnp.int32, (rows, cols), 0)
    s = lax.broadcasted_iota(jnp.int32, (rows, cols), 1)
    return jnp.where(source(d) == s, 1.0, 0.0).astype(bf16)


def move(matrix, x):
    return jnp.dot(matrix, x, preferred_element_type=f32).astype(bf16)


def swapped(d):
    return ((d & 15) << 4) | (d >> 4)


def gout_source(d):
    f8, core, x, z, i = d & 7, (d >> 3) & 1, (d >> 4) & 3, (d >> 6) & 1, d >> 7
    r = (x << 2) - 1 + core * GHALF + i
    f = (z << 3) | f8
    inside = (f << 4) + r
    return jnp.where(r < 0, 256 + f, jnp.where(r > 15, 272 + f, inside))


def act_source(d):
    f, r = d >> 4, d & 15
    return ((f >> 3) << 7) | (r << 3) | (f & 7)


def fetch(srcs, dsts, sems):
    copies = [
        pltpu.make_async_copy(src, dst, sems.at[i])
        for i, (src, dst) in enumerate(zip(srcs, dsts))
    ]
    for copy in copies:
        copy.start()
    return copies


def edges(up, skip, gout, down, above, u, k, g, sems):
    copies = fetch((up, skip, gout), (u, k, g), sems)
    n = 2 * OWN
    top = picks(n, OWN * OWN, swapped)
    bottom = picks(n, OWN * OWN, lambda d: swapped(d + OWN * OWN - n))
    for i, ref in enumerate((u, k)):
        copies[i].wait()
        x = ref[...]
        above[i * n : (i + 1) * n, :] = move(top, x)
        down[i * n : (i + 1) * n, :] = move(bottom, x)
    copies[2].wait()
    x = g[...]
    above[2 * n :, :] = move(top[:OWN], x)
    down[2 * n :, :] = move(bottom[OWN:], x)


def by_row(up, skip, gout, w, up_rows, skip_rows, g_out, w_out, u, k, sems):
    copies = fetch((up, skip, gout, w), (u, k, g_out, w_out), sems)
    swap = picks(OWN * OWN, OWN * OWN, swapped)
    for copy, ref, rows in zip(copies, (u, k), (up_rows, skip_rows)):
        copy.wait()
        rows[...] = move(swap, ref[...])
    for copy in copies[2:]:
        copy.wait()


def pack(up_rows, skip_rows, gout, w, before, after, out):
    n = 2 * OWN
    s = lax.axis_index("space")
    before = jnp.where(s > 0, before[...].astype(f32), 0.0).astype(bf16)
    after = jnp.where(s < NY * NH - 1, after[...].astype(f32), 0.0).astype(bf16)
    rows = [
        jnp.concatenate(
            [before[i * n : (i + 1) * n, :], ref[...], after[i * n : (i + 1) * n, :]], 0
        )
        for i, ref in enumerate((up_rows, skip_rows))
    ]
    g = jnp.concatenate([gout[...], before[2 * n :, :], after[2 * n :, :]], 0)
    g = jnp.dot(
        picks(GHALF * PEERS * HALF, OWN * OWN + 2 * OWN, gout_source),
        g,
        preferred_element_type=f32,
    )
    wt = w[...].astype(f32)
    for z in range(NZ):
        for x in range(NX):
            for c in range(NC):
                t = (z * NX + x) * NC + c
                out[t, 0:FEAT, :] = rows[c][x * ROWS * OWN : x * ROWS * OWN + FEAT, :]
                parts = [
                    g[(i * PEERS + t) * HALF : (i * PEERS + t + 1) * HALF]
                    for i in range(GHALF)
                ] + [
                    wt[
                        k * OWN + z * HALF : k * OWN + (z + 1) * HALF,
                        c * W : (c + 1) * W,
                    ]
                    for k in range(TAPS)
                ]
                out[t, FEAT:, :] = jnp.concatenate(parts, 0).astype(bf16)


def column(n=W):
    return lax.broadcasted_iota(jnp.int32, (1, n), 1)


def from_left(x):
    return jnp.where(column() == 0, 0.0, pltpu.roll(x, 1, 1))


def from_right(x):
    return jnp.where(column() == W - 1, 0.0, pltpu.roll(x, W - 1, 1))


def forward(block, part, gout, feat, wback, wfwd):
    for r in range(FROWS):
        for s in range(PEERS):
            at = r * CHAN + s * OWN
            feat[at : at + OWN, :] = block[s, r * OWN : (r + 1) * OWN, :]
    rest = block[:, FEAT:, :].astype(f32)
    for i in range(GHALF):
        piece = rest[:, i * HALF : (i + 1) * HALF, :].reshape(FILT, W)
        gout[i * FILT : (i + 1) * FILT, :] = piece.astype(bf16)
    for p in range(3):
        for q in range(3):
            at = GOUT + (3 * p + q) * HALF
            piece = rest[:, at : at + HALF, :].reshape(FILT, W).astype(bf16)
            wfwd[q * FILT : (q + 1) * FILT, p * W : (p + 1) * W] = piece
            wback[(2 - p) * FILT : (3 - p) * FILT, q * W : (q + 1) * W] = piece
    for r in range(GROWS):
        y = jnp.dot(
            wfwd[...], feat[r * CHAN : (r + 3) * CHAN, :], preferred_element_type=f32
        )
        part[r * FILT : (r + 1) * FILT, :] = (
            from_left(y[:FILT]) + y[FILT : 2 * FILT] + from_right(y[2 * FILT :])
        )


def backward(mine, other, g_mine, g_other, feat, wback, out, gout, grad, rows, acc):
    core = lax.rem(lax.axis_index("chan"), NC)
    n = GHALF * FILT
    gout[pl.ds(pl.multiple_of(core * n, FILT), n), :] = g_mine[...]
    gout[pl.ds(pl.multiple_of((1 - core) * n, FILT), n), :] = g_other[...]
    for r in range(GROWS):
        at = slice(r * FILT, (r + 1) * FILT)
        pre = mine[at, :] + other[at, :]
        s = jax.nn.sigmoid(pre)
        rows[at, :] = pre * s
        g = gout[at, :].astype(f32) * s * (1.0 + pre * (1.0 - s))
        grad[at, :] = g.astype(bf16)
    n = ROWS // NC
    kept = rows[pl.ds(pl.multiple_of((1 + core * n) * FILT, FILT), n * FILT), :]
    kept = kept.reshape(n, PEERS, HALF, W)
    for i in range(n):
        acc[:, i * HALF : (i + 1) * HALF, :] = kept[i]

    for r in range(ROWS):
        y = lax.dot_general(
            wback[...],
            grad[r * FILT : (r + 3) * FILT, :],
            (((0,), (0,)), ((), ())),
            preferred_element_type=f32,
        )
        g = from_right(y[:CHAN]) + y[CHAN : 2 * CHAN] + from_left(y[2 * CHAN :])
        out[:, r * OWN : (r + 1) * OWN, :] = g.astype(bf16).reshape(PEERS, OWN, W)

    g = grad[FILT : (ROWS + 1) * FILT, :].astype(f32)
    sides = []
    for moved in (from_right(g), g, from_left(g)):
        m = moved.astype(bf16)
        sides.append(
            jnp.concatenate([m[r * FILT : (r + 1) * FILT] for r in range(ROWS)], 1)
        )
    sides = jnp.concatenate(sides, 0)
    for p in range(3):
        f = jnp.concatenate(
            [feat[(r + p + 1) * CHAN : (r + p + 2) * CHAN, :] for r in range(ROWS)], 1
        )
        d = lax.dot_general(
            sides, f, (((1,), (1,)), ((), ())), preferred_element_type=f32
        )
        for q in range(3):
            at = ACT + (3 * p + q) * HALF
            acc[:, at : at + HALF, :] = d[q * FILT : (q + 1) * FILT].reshape(
                PEERS, HALF, W
            )
    out[:, GRAD:, :] = acc[...].astype(bf16)


def weight_pieces(block, out):
    lane = lax.broadcasted_iota(jnp.int32, (1, 128), 1)
    spaces = NY * NH
    turned = []
    for c in range(NC):
        totals = []
        for z in range(NZ):
            total = 0.0
            for x in range(NX):
                t = (z * NX + x) * NC + c
                total = total + block[t, GRAD:, :].astype(f32)[ACT:]
            totals.append(total)
        for half in range(2):
            at = slice(half * 128, (half + 1) * 128)
            turned.append(
                [
                    [t[:, at] if k == 0 else pltpu.roll(t[:, at], 32 * k, 1) for k in range(4)]
                    for t in totals
                ]
            )
    for s in range(spaces):
        rows = []
        for i in range(PIECE // 8):
            row = jnp.zeros((8, 128), f32)
            for g in range(4):
                tap, z = divmod(4 * i + g, 2)
                if tap < TAPS:
                    part = turned[s // 4][z][(g - s) % 4][tap * 8 : tap * 8 + 8]
                    row = jnp.where(lane // 32 == g, part, row)
            rows.append(row)
        out[s] = jnp.concatenate(rows, 0).astype(bf16)


def finish(factor, block, pieces, act, grad_up, grad_skip, out):
    swap = picks(OWN * OWN, OWN * OWN, swapped)
    for c, ref in enumerate((grad_up, grad_skip)):
        rows = []
        for x in range(NX):
            t = x * NC + c
            rows.append(
                block[t, :GRAD, :].astype(f32)
                + block[t + NX * NC, :GRAD, :].astype(f32)
            )
        ref[...] = move(swap, jnp.concatenate(rows, 0).astype(bf16))
    a = block[:, GRAD : GRAD + ACT, :].reshape(PEERS * ACT, W)
    act[...] = move(picks(OWN * OWN, OWN * OWN, act_source), a)

    t = pieces[0].astype(f32)
    for s in range(1, NY * NH):
        t = t + pieces[s].astype(f32)
    t = t * factor
    for g in range(4):
        part = (t if g == 0 else pltpu.roll(t, 128 - 32 * g, 1))[:, :32]
        for i in range(PIECE // 8):
            k = 4 * i + g
            if k < GROUPS:
                out[k * 8 : k * 8 + 8, :] = part[i * 8 : i * 8 + 8]


def shards(upsampled, skip_features, conv_weight, grad_output):
    tiles = lax.axis_size("space")
    width = grad_output.shape[3]
    factor = 1.0 / math.sqrt(grad_output.shape[1] * grad_output.shape[2] * tiles * width)

    down = [(i, (i + 1) % tiles) for i in range(tiles)]
    up = [(j, i) for i, j in down]

    n = OWN * OWN
    anywhere = pl.BlockSpec(memory_space=pltpu.HBM)
    raw = [
        pltpu.with_memory_space_constraint(x, pltpu.HBM)
        for x in (
            upsampled.reshape(n, W),
            skip_features.reshape(n, W),
            grad_output.reshape(n, W),
            conv_weight.transpose(1, 0, 2).reshape(TAPS * OWN, 2 * W),
        )
    ]
    first, last = call(
        edges,
        [pltpu.VMEM((EDGE, W), bf16)] * 2,
        [((n, W), bf16)] * 3 + [pltpu.SemaphoreType.DMA((3,))],
        in_specs=[anywhere] * 3,
    )(*raw[:3])
    before = lax.ppermute(first, "space", down)
    after = lax.ppermute(last, "space", up)
    held = call(
        by_row,
        [((n, W), bf16)] * 3 + [((TAPS * OWN, 2 * W), bf16)],
        [((n, W), bf16)] * 2 + [pltpu.SemaphoreType.DMA((4,))],
        in_specs=[anywhere] * 4,
    )(*raw)
    (sent,) = call(pack, [((PEERS, IN_BLOCK, W), bf16)])(*held, before, after)
    block = lax.all_to_all(sent, "chan", 0, 0, tiled=True)
    part, gout, feat, wback = call(
        forward,
        [
            ((GROWS * FILT, W), f32),
            ((GHALF * FILT, W), bf16),
            ((FROWS * CHAN, W), bf16),
            ((3 * FILT, 3 * W), bf16),
        ],
        [((3 * FILT, 3 * W), bf16)],
    )(block)
    pair = [(i, i ^ 1) for i in range(PEERS)]
    (sent,) = call(
        backward,
        [((PEERS, OUT_BLOCK, W), bf16)],
        [
            ((GROWS * FILT, W), bf16),
            ((GROWS * FILT, W), bf16),
            ((GROWS * FILT, W), f32),
            ((PEERS, OUT_BLOCK - GRAD, W), f32),
        ],
    )(
        part,
        lax.ppermute(part, "chan", pair),
        gout,
        lax.ppermute(gout, "chan", pair),
        feat,
        wback,
    )
    block = lax.all_to_all(sent, "chan", 0, 0, tiled=True)

    (pieces,) = call(weight_pieces, [((tiles, PIECE, 128), bf16)])(block)
    pieces = lax.all_to_all(pieces, "space", 0, 0, tiled=True)
    activation, grad_up, grad_skip, wgrad = call(
        functools.partial(finish, factor),
        [((n, W), bf16)] * 3 + [((TAPS * OWN, 32), f32)],
    )(block, pieces)
    shape = upsampled.shape
    return (
        activation.reshape(shape),
        grad_up.reshape(shape),
        grad_skip.reshape(shape),
        wgrad.reshape(TAPS, OWN, 32).transpose(1, 0, 2),
    )


def solution(mesh):
    tile = P("chan", None, "space", None)
    in_specs = (tile, tile, P("chan", None, None), tile)
    out_specs = (tile, tile, tile, P("chan", None, "space"))
    return jax.shard_map(
        shards, mesh=mesh, in_specs=in_specs, out_specs=out_specs, check_vma=False
    )
```

```python
import functools
import math

import jax
import jax.numpy as jnp
from jax import lax
from jax.experimental import pallas as pl
from jax.experimental.pallas import tpu as pltpu
from jax.sharding import PartitionSpec as P

NZ, NX, NC = 2, 4, 2
PEERS = NZ * NX * NC
NY, NH = 4, 4
W = 256
OWN = 16
HALF = OWN // NZ
ROWS = OWN // NX
FILT = PEERS * HALF
CHAN = PEERS * OWN
TAPS = 9

FROWS = ROWS + 4
GROWS = ROWS + 2
FEAT = FROWS * OWN
GHALF = GROWS // NC
GOUT = GHALF * HALF
IN_BLOCK = FEAT + GOUT + TAPS * HALF
EDGE = 2 * 2 * OWN + OWN
GRAD = ROWS * OWN
ACT = (ROWS // NC) * HALF
OUT_BLOCK = GRAD + ACT + TAPS * HALF
GROUPS = TAPS * OWN // 8
PIECE = -(-GROUPS // 4) * 8

bf16 = jnp.bfloat16
f32 = jnp.float32


def call(body, outs, scratch=(), in_specs=None, vmem=32):
    specs = {} if in_specs is None else {"in_specs": in_specs}
    return pl.pallas_call(
        body,
        out_shape=[jax.ShapeDtypeStruct(*s) if isinstance(s, tuple) else s for s in outs],
        scratch_shapes=[pltpu.VMEM(*s) if isinstance(s, tuple) else s for s in scratch],
        compiler_params=pltpu.CompilerParams(vmem_limit_bytes=vmem * 1024 * 1024),
        **specs,
    )


def picks(rows, cols, source):
    d = lax.broadcasted_iota(jnp.int32, (rows, cols), 0)
    s = lax.broadcasted_iota(jnp.int32, (rows, cols), 1)
    return jnp.where(source(d) == s, 1.0, 0.0).astype(bf16)


def move(matrix, x):
    return jnp.dot(matrix, x, preferred_element_type=f32).astype(bf16)


def swapped(d):
    return ((d & 15) << 4) | (d >> 4)


def gout_source(d):
    f8, core, x, z, i = d & 7, (d >> 3) & 1, (d >> 4) & 3, (d >> 6) & 1, d >> 7
    r = (x << 2) - 1 + core * GHALF + i
    f = (z << 3) | f8
    inside = (f << 4) + r
    return jnp.where(r < 0, 256 + f, jnp.where(r > 15, 272 + f, inside))


def act_source(d):
    f, r = d >> 4, d & 15
    return ((f >> 3) << 7) | (r << 3) | (f & 7)


def fetch(srcs, dsts, sems):
    copies = [
        pltpu.make_async_copy(src, dst, sems.at[i])
        for i, (src, dst) in enumerate(zip(srcs, dsts))
    ]
    for copy in copies:
        copy.start()
    return copies


def edges(up, skip, gout, down, above, u, k, g, sems):
    copies = fetch((up, skip, gout), (u, k, g), sems)
    n = 2 * OWN
    top = picks(n, OWN * OWN, swapped)
    bottom = picks(n, OWN * OWN, lambda d: swapped(d + OWN * OWN - n))
    for i, ref in enumerate((u, k)):
        copies[i].wait()
        x = ref[...]
        above[i * n : (i + 1) * n, :] = move(top, x)
        down[i * n : (i + 1) * n, :] = move(bottom, x)
    copies[2].wait()
    x = g[...]
    above[2 * n :, :] = move(top[:OWN], x)
    down[2 * n :, :] = move(bottom[OWN:], x)


def by_row(up, skip, gout, w, up_rows, skip_rows, g_out, w_out, u, k, sems):
    copies = fetch((up, skip, gout, w), (u, k, g_out, w_out), sems)
    swap = picks(OWN * OWN, OWN * OWN, swapped)
    for copy, ref, rows in zip(copies, (u, k), (up_rows, skip_rows)):
        copy.wait()
        rows[...] = move(swap, ref[...])
    for copy in copies[2:]:
        copy.wait()


def pack(up_rows, skip_rows, gout, w, before, after, out):
    n = 2 * OWN
    s = lax.axis_index("space")
    before = jnp.where(s > 0, before[...].astype(f32), 0.0).astype(bf16)
    after = jnp.where(s < NY * NH - 1, after[...].astype(f32), 0.0).astype(bf16)
    rows = [
        jnp.concatenate(
            [before[i * n : (i + 1) * n, :], ref[...], after[i * n : (i + 1) * n, :]], 0
        )
        for i, ref in enumerate((up_rows, skip_rows))
    ]
    g = jnp.concatenate([gout[...], before[2 * n :, :], after[2 * n :, :]], 0)
    g = jnp.dot(
        picks(GHALF * PEERS * HALF, OWN * OWN + 2 * OWN, gout_source),
        g,
        preferred_element_type=f32,
    )
    wt = w[...].astype(f32)
    for z in range(NZ):
        for x in range(NX):
            for c in range(NC):
                t = (z * NX + x) * NC + c
                out[t, 0:FEAT, :] = rows[c][x * ROWS * OWN : x * ROWS * OWN + FEAT, :]
                parts = [
                    g[(i * PEERS + t) * HALF : (i * PEERS + t + 1) * HALF]
                    for i in range(GHALF)
                ] + [
                    wt[
                        k * OWN + z * HALF : k * OWN + (z + 1) * HALF,
                        c * W : (c + 1) * W,
                    ]
                    for k in range(TAPS)
                ]
                out[t, FEAT:, :] = jnp.concatenate(parts, 0).astype(bf16)


def column(n=W):
    return lax.broadcasted_iota(jnp.int32, (1, n), 1)


def from_left(x):
    return jnp.where(column() == 0, 0.0, pltpu.roll(x, 1, 1))


def from_right(x):
    return jnp.where(column() == W - 1, 0.0, pltpu.roll(x, W - 1, 1))


def forward(block, part, short, gout, feat, wback, wfwd):
    for r in range(FROWS):
        for s in range(PEERS):
            at = r * CHAN + s * OWN
            feat[at : at + OWN, :] = block[s, r * OWN : (r + 1) * OWN, :]
    rest = block[:, FEAT:, :].astype(f32)
    for i in range(GHALF):
        piece = rest[:, i * HALF : (i + 1) * HALF, :].reshape(FILT, W)
        gout[i * FILT : (i + 1) * FILT, :] = piece.astype(bf16)
    for p in range(3):
        for q in range(3):
            at = GOUT + (3 * p + q) * HALF
            piece = rest[:, at : at + HALF, :].reshape(FILT, W).astype(bf16)
            wfwd[q * FILT : (q + 1) * FILT, p * W : (p + 1) * W] = piece
            wback[(2 - p) * FILT : (3 - p) * FILT, q * W : (q + 1) * W] = piece
    for r in range(GROWS):
        y = jnp.dot(
            wfwd[...], feat[r * CHAN : (r + 3) * CHAN, :], preferred_element_type=f32
        )
        y = from_left(y[:FILT]) + y[FILT : 2 * FILT] + from_right(y[2 * FILT :])
        part[r * FILT : (r + 1) * FILT, :] = y
        short[r * FILT : (r + 1) * FILT, :] = y.astype(bf16)


def backward(mine, other, g_mine, g_other, feat, wback, out, gout, grad, rows, acc):
    core = lax.rem(lax.axis_index("chan"), NC)
    n = GHALF * FILT
    gout[pl.ds(pl.multiple_of(core * n, FILT), n), :] = g_mine[...]
    gout[pl.ds(pl.multiple_of((1 - core) * n, FILT), n), :] = g_other[...]
    for r in range(GROWS):
        at = slice(r * FILT, (r + 1) * FILT)
        pre = mine[at, :] + other[at, :].astype(f32)
        s = jax.nn.sigmoid(pre)
        rows[at, :] = pre * s
        g = gout[at, :].astype(f32) * s * (1.0 + pre * (1.0 - s))
        grad[at, :] = g.astype(bf16)
    n = ROWS // NC
    kept = rows[pl.ds(pl.multiple_of((1 + core * n) * FILT, FILT), n * FILT), :]
    kept = kept.reshape(n, PEERS, HALF, W)
    for i in range(n):
        acc[:, i * HALF : (i + 1) * HALF, :] = kept[i]

    for r in range(ROWS):
        y = lax.dot_general(
            wback[...],
            grad[r * FILT : (r + 3) * FILT, :],
            (((0,), (0,)), ((), ())),
            preferred_element_type=f32,
        )
        g = from_right(y[:CHAN]) + y[CHAN : 2 * CHAN] + from_left(y[2 * CHAN :])
        out[:, r * OWN : (r + 1) * OWN, :] = g.astype(bf16).reshape(PEERS, OWN, W)

    g = grad[FILT : (ROWS + 1) * FILT, :].astype(f32)
    sides = []
    for moved in (from_right(g), g, from_left(g)):
        m = moved.astype(bf16)
        sides.append(
            jnp.concatenate([m[r * FILT : (r + 1) * FILT] for r in range(ROWS)], 1)
        )
    sides = jnp.concatenate(sides, 0)
    for p in range(3):
        f = jnp.concatenate(
            [feat[(r + p + 1) * CHAN : (r + p + 2) * CHAN, :] for r in range(ROWS)], 1
        )
        d = lax.dot_general(
            sides, f, (((1,), (1,)), ((), ())), preferred_element_type=f32
        )
        for q in range(3):
            at = ACT + (3 * p + q) * HALF
            acc[:, at : at + HALF, :] = d[q * FILT : (q + 1) * FILT].reshape(
                PEERS, HALF, W
            )
    out[:, GRAD:, :] = acc[...].astype(bf16)


def weight_pieces(block, out):
    lane = lax.broadcasted_iota(jnp.int32, (1, 128), 1)
    spaces = NY * NH
    turned = []
    for c in range(NC):
        totals = []
        for z in range(NZ):
            total = 0.0
            for x in range(NX):
                t = (z * NX + x) * NC + c
                total = total + block[t, GRAD:, :].astype(f32)[ACT:]
            totals.append(total)
        for half in range(2):
            at = slice(half * 128, (half + 1) * 128)
            turned.append(
                [
                    [t[:, at] if k == 0 else pltpu.roll(t[:, at], 32 * k, 1) for k in range(4)]
                    for t in totals
                ]
            )
    for s in range(spaces):
        rows = []
        for i in range(PIECE // 8):
            row = jnp.zeros((8, 128), f32)
            for g in range(4):
                tap, z = divmod(4 * i + g, 2)
                if tap < TAPS:
                    part = turned[s // 4][z][(g - s) % 4][tap * 8 : tap * 8 + 8]
                    row = jnp.where(lane // 32 == g, part, row)
            rows.append(row)
        out[s] = jnp.concatenate(rows, 0).astype(bf16)


def finish(factor, block, pieces, act, grad_up, grad_skip, out):
    swap = picks(OWN * OWN, OWN * OWN, swapped)
    for c, ref in enumerate((grad_up, grad_skip)):
        rows = []
        for x in range(NX):
            t = x * NC + c
            rows.append(
                block[t, :GRAD, :].astype(f32)
                + block[t + NX * NC, :GRAD, :].astype(f32)
            )
        ref[...] = move(swap, jnp.concatenate(rows, 0).astype(bf16))
    a = block[:, GRAD : GRAD + ACT, :].reshape(PEERS * ACT, W)
    act[...] = move(picks(OWN * OWN, OWN * OWN, act_source), a)

    t = pieces[0].astype(f32)
    for s in range(1, NY * NH):
        t = t + pieces[s].astype(f32)
    t = t * factor
    for g in range(4):
        part = (t if g == 0 else pltpu.roll(t, 128 - 32 * g, 1))[:, :32]
        for i in range(PIECE // 8):
            k = 4 * i + g
            if k < GROUPS:
                out[k * 8 : k * 8 + 8, :] = part[i * 8 : i * 8 + 8]


def shards(upsampled, skip_features, conv_weight, grad_output):
    tiles = lax.axis_size("space")
    width = grad_output.shape[3]
    factor = 1.0 / math.sqrt(grad_output.shape[1] * grad_output.shape[2] * tiles * width)

    down = [(i, (i + 1) % tiles) for i in range(tiles)]
    up = [(j, i) for i, j in down]

    n = OWN * OWN
    anywhere = pl.BlockSpec(memory_space=pltpu.HBM)
    raw = [
        pltpu.with_memory_space_constraint(x, pltpu.HBM)
        for x in (
            upsampled.reshape(n, W),
            skip_features.reshape(n, W),
            grad_output.reshape(n, W),
            conv_weight.transpose(1, 0, 2).reshape(TAPS * OWN, 2 * W),
        )
    ]
    first, last = call(
        edges,
        [pltpu.VMEM((EDGE, W), bf16)] * 2,
        [((n, W), bf16)] * 3 + [pltpu.SemaphoreType.DMA((3,))],
        in_specs=[anywhere] * 3,
    )(*raw[:3])
    before = lax.ppermute(first, "space", down)
    after = lax.ppermute(last, "space", up)
    held = call(
        by_row,
        [((n, W), bf16)] * 3 + [((TAPS * OWN, 2 * W), bf16)],
        [((n, W), bf16)] * 2 + [pltpu.SemaphoreType.DMA((4,))],
        in_specs=[anywhere] * 4,
    )(*raw)
    (sent,) = call(pack, [((PEERS, IN_BLOCK, W), bf16)])(*held, before, after)
    block = lax.all_to_all(sent, "chan", 0, 0, tiled=True)
    part, short, gout, feat, wback = call(
        forward,
        [
            ((GROWS * FILT, W), f32),
            ((GROWS * FILT, W), bf16),
            ((GHALF * FILT, W), bf16),
            ((FROWS * CHAN, W), bf16),
            ((3 * FILT, 3 * W), bf16),
        ],
        [((3 * FILT, 3 * W), bf16)],
    )(block)
    pair = [(i, i ^ 1) for i in range(PEERS)]
    (sent,) = call(
        backward,
        [((PEERS, OUT_BLOCK, W), bf16)],
        [
            ((GROWS * FILT, W), bf16),
            ((GROWS * FILT, W), bf16),
            ((GROWS * FILT, W), f32),
            ((PEERS, OUT_BLOCK - GRAD, W), f32),
        ],
    )(
        part,
        lax.ppermute(short, "chan", pair),
        gout,
        lax.ppermute(gout, "chan", pair),
        feat,
        wback,
    )
    block = lax.all_to_all(sent, "chan", 0, 0, tiled=True)

    (pieces,) = call(weight_pieces, [((tiles, PIECE, 128), bf16)])(block)
    pieces = lax.all_to_all(pieces, "space", 0, 0, tiled=True)
    activation, grad_up, grad_skip, wgrad = call(
        functools.partial(finish, factor),
        [((n, W), bf16)] * 3 + [((TAPS * OWN, 32), f32)],
    )(block, pieces)
    shape = upsampled.shape
    return (
        activation.reshape(shape),
        grad_up.reshape(shape),
        grad_skip.reshape(shape),
        wgrad.reshape(TAPS, OWN, 32).transpose(1, 0, 2),
    )


def solution(mesh):
    tile = P("chan", None, "space", None)
    in_specs = (tile, tile, P("chan", None, None), tile)
    out_specs = (tile, tile, tile, P("chan", None, "space"))
    return jax.shard_map(
        shards, mesh=mesh, in_specs=in_specs, out_specs=out_specs, check_vma=False
    )
```

```python
import functools
import math

import jax
import jax.numpy as jnp
from jax import lax
from jax.experimental import pallas as pl
from jax.experimental.pallas import tpu as pltpu
from jax.sharding import PartitionSpec as P

NZ, NX, NC = 2, 4, 2
PEERS = NZ * NX * NC
NY, NH = 4, 4
W = 256
OWN = 16
HALF = OWN // NZ
ROWS = OWN // NX
FILT = PEERS * HALF
CHAN = PEERS * OWN
TAPS = 9

FROWS = ROWS + 4
GROWS = ROWS + 2
FEAT = FROWS * OWN
GHALF = GROWS // NC
GOUT = GHALF * HALF
IN_BLOCK = FEAT + GOUT + TAPS * HALF
EDGE = 2 * 2 * OWN + OWN
GRAD = ROWS * OWN
ACT = (ROWS // NC) * HALF
OUT_BLOCK = GRAD + ACT + TAPS * HALF
GROUPS = TAPS * OWN // 8
PIECE = -(-GROUPS // 4) * 8

bf16 = jnp.bfloat16
f32 = jnp.float32


def call(body, outs, scratch=(), in_specs=None, vmem=32):
    specs = {} if in_specs is None else {"in_specs": in_specs}
    return pl.pallas_call(
        body,
        out_shape=[jax.ShapeDtypeStruct(*s) if isinstance(s, tuple) else s for s in outs],
        scratch_shapes=[pltpu.VMEM(*s) if isinstance(s, tuple) else s for s in scratch],
        compiler_params=pltpu.CompilerParams(vmem_limit_bytes=vmem * 1024 * 1024),
        **specs,
    )


def picks(rows, cols, source):
    d = lax.broadcasted_iota(jnp.int32, (rows, cols), 0)
    s = lax.broadcasted_iota(jnp.int32, (rows, cols), 1)
    return jnp.where(source(d) == s, 1.0, 0.0).astype(bf16)


def move(matrix, x):
    return jnp.dot(matrix, x, preferred_element_type=f32).astype(bf16)


def swapped(d):
    return ((d & 15) << 4) | (d >> 4)


def gout_source(d):
    f8, core, x, z, i = d & 7, (d >> 3) & 1, (d >> 4) & 3, (d >> 6) & 1, d >> 7
    r = (x << 2) - 1 + core * GHALF + i
    f = (z << 3) | f8
    inside = (f << 4) + r
    return jnp.where(r < 0, 256 + f, jnp.where(r > 15, 272 + f, inside))


def act_source(d):
    f, r = d >> 4, d & 15
    return ((f >> 3) << 7) | (r << 3) | (f & 7)


def fetch(srcs, dsts, sems):
    copies = [
        pltpu.make_async_copy(src, dst, sems.at[i])
        for i, (src, dst) in enumerate(zip(srcs, dsts))
    ]
    for copy in copies:
        copy.start()
    return copies


def edges(up, skip, gout, one, two, u, k, g, sems):
    copies = fetch((up, skip, gout), (u, k, g), sems)
    odd = lax.rem(lax.axis_index("space"), 2) == 1
    n = 2 * OWN
    top = swapped
    bottom = lambda d: swapped(d + OWN * OWN - n)
    near = picks(n, OWN * OWN, lambda d: jnp.where(odd, top(d), bottom(d)))
    far = picks(n, OWN * OWN, lambda d: jnp.where(odd, bottom(d), top(d)))
    near_g = picks(OWN, OWN * OWN, lambda d: (d << 4) + jnp.where(odd, 0, OWN - 1))
    far_g = picks(OWN, OWN * OWN, lambda d: (d << 4) + jnp.where(odd, OWN - 1, 0))
    for i, ref in enumerate((u, k)):
        copies[i].wait()
        x = ref[...]
        one[i * n : (i + 1) * n, :] = move(near, x)
        two[i * n : (i + 1) * n, :] = move(far, x)
    copies[2].wait()
    x = g[...]
    one[2 * n :, :] = move(near_g, x)
    two[2 * n :, :] = move(far_g, x)


def by_row(up, skip, gout, w, up_rows, skip_rows, g_out, w_out, u, k, sems):
    copies = fetch((up, skip, gout, w), (u, k, g_out, w_out), sems)
    swap = picks(OWN * OWN, OWN * OWN, swapped)
    for copy, ref, rows in zip(copies, (u, k), (up_rows, skip_rows)):
        copy.wait()
        rows[...] = move(swap, ref[...])
    for copy in copies[2:]:
        copy.wait()


def pack(up_rows, skip_rows, gout, w, one, two, three, out):
    n = 2 * OWN
    s = lax.axis_index("space")
    odd = lax.rem(s, 2) == 1
    near = jnp.where(lax.rem(s, NH) < 2, one[...].astype(f32), three[...].astype(f32))
    far = jnp.where((s > 0) & (s < NY * NH - 1), two[...].astype(f32), 0.0)
    before = jnp.where(odd, near, far).astype(bf16)
    after = jnp.where(odd, far, near).astype(bf16)
    rows = [
        jnp.concatenate(
            [before[i * n : (i + 1) * n, :], ref[...], after[i * n : (i + 1) * n, :]], 0
        )
        for i, ref in enumerate((up_rows, skip_rows))
    ]
    g = jnp.concatenate([gout[...], before[2 * n :, :], after[2 * n :, :]], 0)
    g = jnp.dot(
        picks(GHALF * PEERS * HALF, OWN * OWN + 2 * OWN, gout_source),
        g,
        preferred_element_type=f32,
    )
    wt = w[...].astype(f32)
    for z in range(NZ):
        for x in range(NX):
            for c in range(NC):
                t = (z * NX + x) * NC + c
                out[t, 0:FEAT, :] = rows[c][x * ROWS * OWN : x * ROWS * OWN + FEAT, :]
                parts = [
                    g[(i * PEERS + t) * HALF : (i * PEERS + t + 1) * HALF]
                    for i in range(GHALF)
                ] + [
                    wt[
                        k * OWN + z * HALF : k * OWN + (z + 1) * HALF,
                        c * W : (c + 1) * W,
                    ]
                    for k in range(TAPS)
                ]
                out[t, FEAT:, :] = jnp.concatenate(parts, 0).astype(bf16)


def column(n=W):
    return lax.broadcasted_iota(jnp.int32, (1, n), 1)


def from_left(x):
    return jnp.where(column() == 0, 0.0, pltpu.roll(x, 1, 1))


def from_right(x):
    return jnp.where(column() == W - 1, 0.0, pltpu.roll(x, W - 1, 1))


def forward(block, part, short, gout, feat, wback, wfwd):
    for r in range(FROWS):
        for s in range(PEERS):
            at = r * CHAN + s * OWN
            feat[at : at + OWN, :] = block[s, r * OWN : (r + 1) * OWN, :]
    rest = block[:, FEAT:, :].astype(f32)
    for i in range(GHALF):
        piece = rest[:, i * HALF : (i + 1) * HALF, :].reshape(FILT, W)
        gout[i * FILT : (i + 1) * FILT, :] = piece.astype(bf16)
    for p in range(3):
        for q in range(3):
            at = GOUT + (3 * p + q) * HALF
            piece = rest[:, at : at + HALF, :].reshape(FILT, W).astype(bf16)
            wfwd[q * FILT : (q + 1) * FILT, p * W : (p + 1) * W] = piece
            wback[(2 - p) * FILT : (3 - p) * FILT, q * W : (q + 1) * W] = piece
    for r in range(GROWS):
        y = jnp.dot(
            wfwd[...], feat[r * CHAN : (r + 3) * CHAN, :], preferred_element_type=f32
        )
        y = from_left(y[:FILT]) + y[FILT : 2 * FILT] + from_right(y[2 * FILT :])
        part[r * FILT : (r + 1) * FILT, :] = y
        short[r * FILT : (r + 1) * FILT, :] = y.astype(bf16)


def backward(mine, other, g_mine, g_other, feat, wback, out, gout, grad, rows, acc):
    core = lax.rem(lax.axis_index("chan"), NC)
    n = GHALF * FILT
    gout[pl.ds(pl.multiple_of(core * n, FILT), n), :] = g_mine[...]
    gout[pl.ds(pl.multiple_of((1 - core) * n, FILT), n), :] = g_other[...]
    for r in range(GROWS):
        at = slice(r * FILT, (r + 1) * FILT)
        pre = mine[at, :] + other[at, :].astype(f32)
        s = jax.nn.sigmoid(pre)
        rows[at, :] = pre * s
        g = gout[at, :].astype(f32) * s * (1.0 + pre * (1.0 - s))
        grad[at, :] = g.astype(bf16)
    n = ROWS // NC
    kept = rows[pl.ds(pl.multiple_of((1 + core * n) * FILT, FILT), n * FILT), :]
    kept = kept.reshape(n, PEERS, HALF, W)
    for i in range(n):
        acc[:, i * HALF : (i + 1) * HALF, :] = kept[i]

    for r in range(ROWS):
        y = lax.dot_general(
            wback[...],
            grad[r * FILT : (r + 3) * FILT, :],
            (((0,), (0,)), ((), ())),
            preferred_element_type=f32,
        )
        g = from_right(y[:CHAN]) + y[CHAN : 2 * CHAN] + from_left(y[2 * CHAN :])
        out[:, r * OWN : (r + 1) * OWN, :] = g.astype(bf16).reshape(PEERS, OWN, W)

    g = grad[FILT : (ROWS + 1) * FILT, :].astype(f32)
    sides = []
    for moved in (from_right(g), g, from_left(g)):
        m = moved.astype(bf16)
        sides.append(
            jnp.concatenate([m[r * FILT : (r + 1) * FILT] for r in range(ROWS)], 1)
        )
    sides = jnp.concatenate(sides, 0)
    for p in range(3):
        f = jnp.concatenate(
            [feat[(r + p + 1) * CHAN : (r + p + 2) * CHAN, :] for r in range(ROWS)], 1
        )
        d = lax.dot_general(
            sides, f, (((1,), (1,)), ((), ())), preferred_element_type=f32
        )
        for q in range(3):
            at = ACT + (3 * p + q) * HALF
            acc[:, at : at + HALF, :] = d[q * FILT : (q + 1) * FILT].reshape(
                PEERS, HALF, W
            )
    out[:, GRAD:, :] = acc[...].astype(bf16)


def weight_pieces(block, out):
    lane = lax.broadcasted_iota(jnp.int32, (1, 128), 1)
    spaces = NY * NH
    turned = []
    for c in range(NC):
        totals = []
        for z in range(NZ):
            total = 0.0
            for x in range(NX):
                t = (z * NX + x) * NC + c
                total = total + block[t, GRAD:, :].astype(f32)[ACT:]
            totals.append(total)
        for half in range(2):
            at = slice(half * 128, (half + 1) * 128)
            turned.append(
                [
                    [t[:, at] if k == 0 else pltpu.roll(t[:, at], 32 * k, 1) for k in range(4)]
                    for t in totals
                ]
            )
    for s in range(spaces):
        rows = []
        for i in range(PIECE // 8):
            row = jnp.zeros((8, 128), f32)
            for g in range(4):
                tap, z = divmod(4 * i + g, 2)
                if tap < TAPS:
                    part = turned[s // 4][z][(g - s) % 4][tap * 8 : tap * 8 + 8]
                    row = jnp.where(lane // 32 == g, part, row)
            rows.append(row)
        out[s] = jnp.concatenate(rows, 0).astype(bf16)


def finish(factor, block, pieces, act, grad_up, grad_skip, out):
    swap = picks(OWN * OWN, OWN * OWN, swapped)
    for c, ref in enumerate((grad_up, grad_skip)):
        rows = []
        for x in range(NX):
            t = x * NC + c
            rows.append(
                block[t, :GRAD, :].astype(f32)
                + block[t + NX * NC, :GRAD, :].astype(f32)
            )
        ref[...] = move(swap, jnp.concatenate(rows, 0).astype(bf16))
    a = block[:, GRAD : GRAD + ACT, :].reshape(PEERS * ACT, W)
    act[...] = move(picks(OWN * OWN, OWN * OWN, act_source), a)

    t = pieces[0].astype(f32)
    for s in range(1, NY * NH):
        t = t + pieces[s].astype(f32)
    t = t * factor
    for g in range(4):
        part = (t if g == 0 else pltpu.roll(t, 128 - 32 * g, 1))[:, :32]
        for i in range(PIECE // 8):
            k = 4 * i + g
            if k < GROUPS:
                out[k * 8 : k * 8 + 8, :] = part[i * 8 : i * 8 + 8]


def shards(upsampled, skip_features, conv_weight, grad_output):
    tiles = lax.axis_size("space")
    width = grad_output.shape[3]
    factor = 1.0 / math.sqrt(grad_output.shape[1] * grad_output.shape[2] * tiles * width)

    def turn(partner):
        pairs = []
        for c in range(PEERS):
            for s in range(tiles):
                p = partner(s)
                to = (c, p) if p is not None else (c ^ 1, s)
                pairs.append((c * tiles + s, to[0] * tiles + to[1]))
        return pairs

    def first_pairs(s):
        return s ^ 1 if s % NH < 2 else None

    def middle_pairs(s):
        p = s + 1 if s % 2 else s - 1
        return p if 0 <= p < tiles else None

    def last_pairs(s):
        return s ^ 1 if s % NH >= 2 else None

    n = OWN * OWN
    anywhere = pl.BlockSpec(memory_space=pltpu.HBM)
    raw = [
        pltpu.with_memory_space_constraint(x, pltpu.HBM)
        for x in (
            upsampled.reshape(n, W),
            skip_features.reshape(n, W),
            grad_output.reshape(n, W),
            conv_weight.transpose(1, 0, 2).reshape(TAPS * OWN, 2 * W),
        )
    ]
    first, last = call(
        edges,
        [pltpu.VMEM((EDGE, W), bf16)] * 2,
        [((n, W), bf16)] * 3 + [pltpu.SemaphoreType.DMA((3,))],
        in_specs=[anywhere] * 3,
    )(*raw[:3])
    both = ("chan", "space")
    halos = (
        lax.ppermute(first, both, turn(first_pairs)),
        lax.ppermute(last, both, turn(middle_pairs)),
        lax.ppermute(first, both, turn(last_pairs)),
    )
    held = call(
        by_row,
        [((n, W), bf16)] * 3 + [((TAPS * OWN, 2 * W), bf16)],
        [((n, W), bf16)] * 2 + [pltpu.SemaphoreType.DMA((4,))],
        in_specs=[anywhere] * 4,
    )(*raw)
    (sent,) = call(pack, [((PEERS, IN_BLOCK, W), bf16)])(*held, *halos)
    block = lax.all_to_all(sent, "chan", 0, 0, tiled=True)
    part, short, gout, feat, wback = call(
        forward,
        [
            ((GROWS * FILT, W), f32),
            ((GROWS * FILT, W), bf16),
            ((GHALF * FILT, W), bf16),
            ((FROWS * CHAN, W), bf16),
            ((3 * FILT, 3 * W), bf16),
        ],
        [((3 * FILT, 3 * W), bf16)],
    )(block)
    pair = [(i, i ^ 1) for i in range(PEERS)]
    (sent,) = call(
        backward,
        [((PEERS, OUT_BLOCK, W), bf16)],
        [
            ((GROWS * FILT, W), bf16),
            ((GROWS * FILT, W), bf16),
            ((GROWS * FILT, W), f32),
            ((PEERS, OUT_BLOCK - GRAD, W), f32),
        ],
    )(
        part,
        lax.ppermute(short, "chan", pair),
        gout,
        lax.ppermute(gout, "chan", pair),
        feat,
        wback,
    )
    block = lax.all_to_all(sent, "chan", 0, 0, tiled=True)

    (pieces,) = call(weight_pieces, [((tiles, PIECE, 128), bf16)])(block)
    pieces = lax.all_to_all(pieces, "space", 0, 0, tiled=True)
    activation, grad_up, grad_skip, wgrad = call(
        functools.partial(finish, factor),
        [((n, W), bf16)] * 3 + [((TAPS * OWN, 32), f32)],
    )(block, pieces)
    shape = upsampled.shape
    return (
        activation.reshape(shape),
        grad_up.reshape(shape),
        grad_skip.reshape(shape),
        wgrad.reshape(TAPS, OWN, 32).transpose(1, 0, 2),
    )


def solution(mesh):
    tile = P("chan", None, "space", None)
    in_specs = (tile, tile, P("chan", None, None), tile)
    out_specs = (tile, tile, tile, P("chan", None, "space"))
    return jax.shard_map(
        shards, mesh=mesh, in_specs=in_specs, out_specs=out_specs, check_vma=False
    )
```

```python
import functools
import math

import jax
import jax.numpy as jnp
from jax import lax
from jax.experimental import pallas as pl
from jax.experimental.pallas import tpu as pltpu
from jax.sharding import PartitionSpec as P

NZ, NX, NC = 2, 4, 2
PEERS = NZ * NX * NC
NY, NH = 4, 4
W = 256
OWN = 16
HALF = OWN // NZ
ROWS = OWN // NX
FILT = PEERS * HALF
CHAN = PEERS * OWN
TAPS = 9

FROWS = ROWS + 4
GROWS = ROWS + 2
FEAT = FROWS * OWN
GHALF = GROWS // NC
GOUT = GHALF * HALF
IN_BLOCK = FEAT + GOUT + TAPS * HALF
EDGE = 2 * 2 * OWN + OWN
GRAD = ROWS * OWN
ACT = (ROWS // NC) * HALF
OUT_BLOCK = GRAD + ACT + TAPS * HALF
GROUPS = TAPS * OWN // 8
PIECE = -(-GROUPS // 4) * 8

bf16 = jnp.bfloat16
f32 = jnp.float32


def call(body, outs, scratch=(), in_specs=None, vmem=32):
    specs = {} if in_specs is None else {"in_specs": in_specs}
    return pl.pallas_call(
        body,
        out_shape=[jax.ShapeDtypeStruct(*s) if isinstance(s, tuple) else s for s in outs],
        scratch_shapes=[pltpu.VMEM(*s) if isinstance(s, tuple) else s for s in scratch],
        compiler_params=pltpu.CompilerParams(vmem_limit_bytes=vmem * 1024 * 1024),
        **specs,
    )


def picks(rows, cols, source):
    d = lax.broadcasted_iota(jnp.int32, (rows, cols), 0)
    s = lax.broadcasted_iota(jnp.int32, (rows, cols), 1)
    return jnp.where(source(d) == s, 1.0, 0.0).astype(bf16)


def move(matrix, x):
    return jnp.dot(matrix, x, preferred_element_type=f32).astype(bf16)


def swapped(d):
    return ((d & 15) << 4) | (d >> 4)


def gout_source(d):
    f8, core, x, z, i = d & 7, (d >> 3) & 1, (d >> 4) & 3, (d >> 6) & 1, d >> 7
    r = (x << 2) - 1 + core * GHALF + i
    f = (z << 3) | f8
    inside = (f << 4) + r
    return jnp.where(r < 0, 256 + f, jnp.where(r > 15, 272 + f, inside))


def act_source(d):
    f, r = d >> 4, d & 15
    return ((f >> 3) << 7) | (r << 3) | (f & 7)


def fetch(srcs, dsts, sems):
    copies = [
        pltpu.make_async_copy(src, dst, sems.at[i])
        for i, (src, dst) in enumerate(zip(srcs, dsts))
    ]
    for copy in copies:
        copy.start()
    return copies


def edges(up, skip, gout, two, one, u, k, g, sems):
    copies = fetch((up, skip, gout), (u, k, g), sems)
    odd = lax.rem(lax.axis_index("space"), 2) == 1
    n = 2 * OWN
    top = swapped
    bottom = lambda d: swapped(d + OWN * OWN - n)
    near = picks(n, OWN * OWN, lambda d: jnp.where(odd, top(d), bottom(d)))
    far = picks(n, OWN * OWN, lambda d: jnp.where(odd, bottom(d), top(d)))
    near_g = picks(OWN, OWN * OWN, lambda d: (d << 4) + jnp.where(odd, 0, OWN - 1))
    far_g = picks(OWN, OWN * OWN, lambda d: (d << 4) + jnp.where(odd, OWN - 1, 0))
    for i, ref in enumerate((u, k)):
        copies[i].wait()
        x = ref[...]
        one[i * n : (i + 1) * n, :] = move(near, x)
        two[i * n : (i + 1) * n, :] = move(far, x)
    copies[2].wait()
    x = g[...]
    one[2 * n :, :] = move(near_g, x)
    two[2 * n :, :] = move(far_g, x)


def by_row(up, skip, gout, w, up_rows, skip_rows, g_out, w_out, u, k, sems):
    copies = fetch((up, skip, gout, w), (u, k, g_out, w_out), sems)
    swap = picks(OWN * OWN, OWN * OWN, swapped)
    for copy, ref, rows in zip(copies, (u, k), (up_rows, skip_rows)):
        copy.wait()
        rows[...] = move(swap, ref[...])
    for copy in copies[2:]:
        copy.wait()


def pack(up_rows, skip_rows, gout, w, two, one, out):
    n = 2 * OWN
    s = lax.axis_index("space")
    odd = lax.rem(s, 2) == 1
    near = one[...].astype(f32)
    far = jnp.where((s > 0) & (s < NY * NH - 1), two[...].astype(f32), 0.0)
    before = jnp.where(odd, near, far).astype(bf16)
    after = jnp.where(odd, far, near).astype(bf16)
    rows = [
        jnp.concatenate(
            [before[i * n : (i + 1) * n, :], ref[...], after[i * n : (i + 1) * n, :]], 0
        )
        for i, ref in enumerate((up_rows, skip_rows))
    ]
    g = jnp.concatenate([gout[...], before[2 * n :, :], after[2 * n :, :]], 0)
    g = jnp.dot(
        picks(GHALF * PEERS * HALF, OWN * OWN + 2 * OWN, gout_source),
        g,
        preferred_element_type=f32,
    )
    wt = w[...].astype(f32)
    for z in range(NZ):
        for x in range(NX):
            for c in range(NC):
                t = (z * NX + x) * NC + c
                out[t, 0:FEAT, :] = rows[c][x * ROWS * OWN : x * ROWS * OWN + FEAT, :]
                parts = [
                    g[(i * PEERS + t) * HALF : (i * PEERS + t + 1) * HALF]
                    for i in range(GHALF)
                ] + [
                    wt[
                        k * OWN + z * HALF : k * OWN + (z + 1) * HALF,
                        c * W : (c + 1) * W,
                    ]
                    for k in range(TAPS)
                ]
                out[t, FEAT:, :] = jnp.concatenate(parts, 0).astype(bf16)


def column(n=W):
    return lax.broadcasted_iota(jnp.int32, (1, n), 1)


def from_left(x):
    return jnp.where(column() == 0, 0.0, pltpu.roll(x, 1, 1))


def from_right(x):
    return jnp.where(column() == W - 1, 0.0, pltpu.roll(x, W - 1, 1))


def forward(block, part, short, gout, feat, wback, wfwd):
    for r in range(FROWS):
        for s in range(PEERS):
            at = r * CHAN + s * OWN
            feat[at : at + OWN, :] = block[s, r * OWN : (r + 1) * OWN, :]
    rest = block[:, FEAT:, :].astype(f32)
    for i in range(GHALF):
        piece = rest[:, i * HALF : (i + 1) * HALF, :].reshape(FILT, W)
        gout[i * FILT : (i + 1) * FILT, :] = piece.astype(bf16)
    for p in range(3):
        for q in range(3):
            at = GOUT + (3 * p + q) * HALF
            piece = rest[:, at : at + HALF, :].reshape(FILT, W).astype(bf16)
            wfwd[q * FILT : (q + 1) * FILT, p * W : (p + 1) * W] = piece
            wback[(2 - p) * FILT : (3 - p) * FILT, q * W : (q + 1) * W] = piece
    for r in range(GROWS):
        y = jnp.dot(
            wfwd[...], feat[r * CHAN : (r + 3) * CHAN, :], preferred_element_type=f32
        )
        y = from_left(y[:FILT]) + y[FILT : 2 * FILT] + from_right(y[2 * FILT :])
        part[r * FILT : (r + 1) * FILT, :] = y
        short[r * FILT : (r + 1) * FILT, :] = y.astype(bf16)


def backward(mine, other, g_mine, g_other, feat, wback, out, gout, grad, rows, acc):
    core = lax.rem(lax.axis_index("chan"), NC)
    n = GHALF * FILT
    gout[pl.ds(pl.multiple_of(core * n, FILT), n), :] = g_mine[...]
    gout[pl.ds(pl.multiple_of((1 - core) * n, FILT), n), :] = g_other[...]
    for r in range(GROWS):
        at = slice(r * FILT, (r + 1) * FILT)
        pre = mine[at, :] + other[at, :].astype(f32)
        s = jax.nn.sigmoid(pre)
        rows[at, :] = pre * s
        g = gout[at, :].astype(f32) * s * (1.0 + pre * (1.0 - s))
        grad[at, :] = g.astype(bf16)
    n = ROWS // NC
    kept = rows[pl.ds(pl.multiple_of((1 + core * n) * FILT, FILT), n * FILT), :]
    kept = kept.reshape(n, PEERS, HALF, W)
    for i in range(n):
        acc[:, i * HALF : (i + 1) * HALF, :] = kept[i]

    for r in range(ROWS):
        y = lax.dot_general(
            wback[...],
            grad[r * FILT : (r + 3) * FILT, :],
            (((0,), (0,)), ((), ())),
            preferred_element_type=f32,
        )
        g = from_right(y[:CHAN]) + y[CHAN : 2 * CHAN] + from_left(y[2 * CHAN :])
        out[:, r * OWN : (r + 1) * OWN, :] = g.astype(bf16).reshape(PEERS, OWN, W)

    g = grad[FILT : (ROWS + 1) * FILT, :].astype(f32)
    sides = []
    for moved in (from_right(g), g, from_left(g)):
        m = moved.astype(bf16)
        sides.append(
            jnp.concatenate([m[r * FILT : (r + 1) * FILT] for r in range(ROWS)], 1)
        )
    sides = jnp.concatenate(sides, 0)
    for p in range(3):
        f = jnp.concatenate(
            [feat[(r + p + 1) * CHAN : (r + p + 2) * CHAN, :] for r in range(ROWS)], 1
        )
        d = lax.dot_general(
            sides, f, (((1,), (1,)), ((), ())), preferred_element_type=f32
        )
        for q in range(3):
            at = ACT + (3 * p + q) * HALF
            acc[:, at : at + HALF, :] = d[q * FILT : (q + 1) * FILT].reshape(
                PEERS, HALF, W
            )
    out[:, GRAD:, :] = acc[...].astype(bf16)


def weight_pieces(block, out):
    lane = lax.broadcasted_iota(jnp.int32, (1, 128), 1)
    spaces = NY * NH
    turned = []
    for c in range(NC):
        totals = []
        for z in range(NZ):
            total = 0.0
            for x in range(NX):
                t = (z * NX + x) * NC + c
                total = total + block[t, GRAD:, :].astype(f32)[ACT:]
            totals.append(total)
        for half in range(2):
            at = slice(half * 128, (half + 1) * 128)
            turned.append(
                [
                    [t[:, at] if k == 0 else pltpu.roll(t[:, at], 32 * k, 1) for k in range(4)]
                    for t in totals
                ]
            )
    for s in range(spaces):
        rows = []
        for i in range(PIECE // 8):
            row = jnp.zeros((8, 128), f32)
            for g in range(4):
                tap, z = divmod(4 * i + g, 2)
                if tap < TAPS:
                    part = turned[s // 4][z][(g - s) % 4][tap * 8 : tap * 8 + 8]
                    row = jnp.where(lane // 32 == g, part, row)
            rows.append(row)
        out[s] = jnp.concatenate(rows, 0).astype(bf16)


def finish(factor, block, pieces, act, grad_up, grad_skip, out):
    swap = picks(OWN * OWN, OWN * OWN, swapped)
    for c, ref in enumerate((grad_up, grad_skip)):
        rows = []
        for x in range(NX):
            t = x * NC + c
            rows.append(
                block[t, :GRAD, :].astype(f32)
                + block[t + NX * NC, :GRAD, :].astype(f32)
            )
        ref[...] = move(swap, jnp.concatenate(rows, 0).astype(bf16))
    a = block[:, GRAD : GRAD + ACT, :].reshape(PEERS * ACT, W)
    act[...] = move(picks(OWN * OWN, OWN * OWN, act_source), a)

    t = pieces[0].astype(f32)
    for s in range(1, NY * NH):
        t = t + pieces[s].astype(f32)
    t = t * factor
    for g in range(4):
        part = (t if g == 0 else pltpu.roll(t, 128 - 32 * g, 1))[:, :32]
        for i in range(PIECE // 8):
            k = 4 * i + g
            if k < GROUPS:
                out[k * 8 : k * 8 + 8, :] = part[i * 8 : i * 8 + 8]


def shards(upsampled, skip_features, conv_weight, grad_output):
    tiles = lax.axis_size("space")
    width = grad_output.shape[3]
    factor = 1.0 / math.sqrt(grad_output.shape[1] * grad_output.shape[2] * tiles * width)

    def turn(partner):
        pairs = []
        for c in range(PEERS):
            for s in range(tiles):
                p = partner(s)
                to = (c, p) if p is not None else (c ^ 1, s)
                pairs.append((c * tiles + s, to[0] * tiles + to[1]))
        return pairs

    def middle_pairs(s):
        p = s + 1 if s % 2 else s - 1
        return p if 0 <= p < tiles else None

    n = OWN * OWN
    anywhere = pl.BlockSpec(memory_space=pltpu.HBM)
    raw = [
        pltpu.with_memory_space_constraint(x, pltpu.HBM)
        for x in (
            upsampled.reshape(n, W),
            skip_features.reshape(n, W),
            grad_output.reshape(n, W),
            conv_weight.transpose(1, 0, 2).reshape(TAPS * OWN, 2 * W),
        )
    ]
    last, first = call(
        edges,
        [pltpu.VMEM((EDGE, W), bf16)] * 2,
        [((n, W), bf16)] * 3 + [pltpu.SemaphoreType.DMA((3,))],
        in_specs=[anywhere] * 3,
    )(*raw[:3])
    both = ("chan", "space")
    halos = (
        lax.ppermute(last, both, turn(middle_pairs)),
        lax.ppermute(first, "space", [(i, i ^ 1) for i in range(tiles)]),
    )
    held = call(
        by_row,
        [((n, W), bf16)] * 3 + [((TAPS * OWN, 2 * W), bf16)],
        [((n, W), bf16)] * 2 + [pltpu.SemaphoreType.DMA((4,))],
        in_specs=[anywhere] * 4,
    )(*raw)
    (sent,) = call(pack, [((PEERS, IN_BLOCK, W), bf16)])(*held, *halos)
    block = lax.all_to_all(sent, "chan", 0, 0, tiled=True)
    part, short, gout, feat, wback = call(
        forward,
        [
            ((GROWS * FILT, W), f32),
            ((GROWS * FILT, W), bf16),
            ((GHALF * FILT, W), bf16),
            ((FROWS * CHAN, W), bf16),
            ((3 * FILT, 3 * W), bf16),
        ],
        [((3 * FILT, 3 * W), bf16)],
    )(block)
    pair = [(i, i ^ 1) for i in range(PEERS)]
    (sent,) = call(
        backward,
        [((PEERS, OUT_BLOCK, W), bf16)],
        [
            ((GROWS * FILT, W), bf16),
            ((GROWS * FILT, W), bf16),
            ((GROWS * FILT, W), f32),
            ((PEERS, OUT_BLOCK - GRAD, W), f32),
        ],
    )(
        part,
        lax.ppermute(short, "chan", pair),
        gout,
        lax.ppermute(gout, "chan", pair),
        feat,
        wback,
    )
    block = lax.all_to_all(sent, "chan", 0, 0, tiled=True)

    (pieces,) = call(weight_pieces, [((tiles, PIECE, 128), bf16)])(block)
    pieces = lax.all_to_all(pieces, "space", 0, 0, tiled=True)
    activation, grad_up, grad_skip, wgrad = call(
        functools.partial(finish, factor),
        [((n, W), bf16)] * 3 + [((TAPS * OWN, 32), f32)],
    )(block, pieces)
    shape = upsampled.shape
    return (
        activation.reshape(shape),
        grad_up.reshape(shape),
        grad_skip.reshape(shape),
        wgrad.reshape(TAPS, OWN, 32).transpose(1, 0, 2),
    )


def solution(mesh):
    tile = P("chan", None, "space", None)
    in_specs = (tile, tile, P("chan", None, None), tile)
    out_specs = (tile, tile, tile, P("chan", None, "space"))
    return jax.shard_map(
        shards, mesh=mesh, in_specs=in_specs, out_specs=out_specs, check_vma=False
    )
```

```python
import functools
import math

import jax
import jax.numpy as jnp
from jax import lax
from jax.experimental import pallas as pl
from jax.experimental.pallas import tpu as pltpu
from jax.sharding import PartitionSpec as P

NZ, NX, NC = 2, 4, 2
PEERS = NZ * NX * NC
NY, NH = 4, 4
W = 256
OWN = 16
HALF = OWN // NZ
ROWS = OWN // NX
FILT = PEERS * HALF
CHAN = PEERS * OWN
TAPS = 9

FROWS = ROWS + 4
GROWS = ROWS + 2
FEAT = FROWS * OWN
GHALF = GROWS // NC
GOUT = GHALF * HALF
IN_BLOCK = FEAT + GOUT + TAPS * HALF
EDGE = 2 * 2 * OWN + OWN
GRAD = ROWS * OWN
ACT = (ROWS // NC) * HALF
OUT_BLOCK = GRAD + ACT + TAPS * HALF
GROUPS = TAPS * OWN // 8
PIECE = -(-GROUPS // 4) * 8

PARTS = 4

bf16 = jnp.bfloat16
f32 = jnp.float32


def call(body, outs, scratch=(), vmem=32, **specs):
    return pl.pallas_call(
        body,
        out_shape=[jax.ShapeDtypeStruct(*s) if isinstance(s, tuple) else s for s in outs],
        scratch_shapes=[pltpu.VMEM(*s) if isinstance(s, tuple) else s for s in scratch],
        compiler_params=pltpu.CompilerParams(vmem_limit_bytes=vmem * 1024 * 1024),
        **specs,
    )


def picks(rows, cols, source):
    d = lax.broadcasted_iota(jnp.int32, (rows, cols), 0)
    s = lax.broadcasted_iota(jnp.int32, (rows, cols), 1)
    return jnp.where(source(d) == s, 1.0, 0.0).astype(bf16)


def move(matrix, x):
    return jnp.dot(matrix, x, preferred_element_type=f32).astype(bf16)


def swapped(d):
    return ((d & 15) << 4) | (d >> 4)


def gout_source(d):
    f8, core, x, z, i = d & 7, (d >> 3) & 1, (d >> 4) & 3, (d >> 6) & 1, d >> 7
    r = (x << 2) - 1 + core * GHALF + i
    f = (z << 3) | f8
    inside = (f << 4) + r
    return jnp.where(r < 0, 256 + f, jnp.where(r > 15, 272 + f, inside))


def act_source(d):
    f, r = d >> 4, d & 15
    return ((f >> 3) << 7) | (r << 3) | (f & 7)


def fetch(srcs, dsts, sems):
    copies = []
    for i, (src, dst) in enumerate(zip(srcs, dsts)):
        n = src.shape[0] // PARTS
        parts = [pl.ds(k * n, n) for k in range(PARTS)]
        copies.append(
            [
                pltpu.make_async_copy(src.at[at], dst.at[at], sems.at[i, k])
                for k, at in enumerate(parts)
            ]
        )
    for parts in copies:
        for copy in parts:
            copy.start()
    return copies


def edges(up, skip, gout, two, one, u, k, g, sems):
    copies = fetch((up, skip, gout), (u, k, g), sems)
    odd = lax.rem(lax.axis_index("space"), 2) == 1
    n = 2 * OWN
    top = swapped
    bottom = lambda d: swapped(d + OWN * OWN - n)
    near = picks(n, OWN * OWN, lambda d: jnp.where(odd, top(d), bottom(d)))
    far = picks(n, OWN * OWN, lambda d: jnp.where(odd, bottom(d), top(d)))
    near_g = picks(OWN, OWN * OWN, lambda d: (d << 4) + jnp.where(odd, 0, OWN - 1))
    far_g = picks(OWN, OWN * OWN, lambda d: (d << 4) + jnp.where(odd, OWN - 1, 0))
    for i, ref in enumerate((u, k)):
        for copy in copies[i]:
            copy.wait()
        x = ref[...]
        one[i * n : (i + 1) * n, :] = move(near, x)
        two[i * n : (i + 1) * n, :] = move(far, x)
    for copy in copies[2]:
        copy.wait()
    x = g[...]
    one[2 * n :, :] = move(near_g, x)
    two[2 * n :, :] = move(far_g, x)


def by_row(up, skip, gout, w, up_rows, skip_rows, g_out, w_out, u, k, sems, w_sem):
    w_copy = pltpu.make_async_copy(w, w_out, w_sem)
    w_copy.start()
    copies = fetch((up, skip, gout), (u, k, g_out), sems)
    swap = picks(OWN * OWN, OWN * OWN, swapped)
    for parts, ref, rows in zip(copies, (u, k), (up_rows, skip_rows)):
        for copy in parts:
            copy.wait()
        rows[...] = move(swap, ref[...])
    for copy in copies[2]:
        copy.wait()
    w_copy.wait()


def pack(up_rows, skip_rows, gout, w, two, one, out):
    n = 2 * OWN
    s = lax.axis_index("space")
    odd = lax.rem(s, 2) == 1
    near = one[...].astype(f32)
    far = jnp.where((s > 0) & (s < NY * NH - 1), two[...].astype(f32), 0.0)
    before = jnp.where(odd, near, far).astype(bf16)
    after = jnp.where(odd, far, near).astype(bf16)
    rows = [
        jnp.concatenate(
            [before[i * n : (i + 1) * n, :], ref[...], after[i * n : (i + 1) * n, :]], 0
        )
        for i, ref in enumerate((up_rows, skip_rows))
    ]
    g = jnp.concatenate([gout[...], before[2 * n :, :], after[2 * n :, :]], 0)
    g = jnp.dot(
        picks(GHALF * PEERS * HALF, OWN * OWN + 2 * OWN, gout_source),
        g,
        preferred_element_type=f32,
    )
    wt = w[...].astype(f32)
    for z in range(NZ):
        for x in range(NX):
            for c in range(NC):
                t = (z * NX + x) * NC + c
                out[t, 0:FEAT, :] = rows[c][x * ROWS * OWN : x * ROWS * OWN + FEAT, :]
                parts = [
                    g[(i * PEERS + t) * HALF : (i * PEERS + t + 1) * HALF]
                    for i in range(GHALF)
                ] + [
                    wt[
                        k * OWN + z * HALF : k * OWN + (z + 1) * HALF,
                        c * W : (c + 1) * W,
                    ]
                    for k in range(TAPS)
                ]
                out[t, FEAT:, :] = jnp.concatenate(parts, 0).astype(bf16)


def column(n=W):
    return lax.broadcasted_iota(jnp.int32, (1, n), 1)


def from_left(x):
    return jnp.where(column() == 0, 0.0, pltpu.roll(x, 1, 1))


def from_right(x):
    return jnp.where(column() == W - 1, 0.0, pltpu.roll(x, W - 1, 1))


def forward(block, part, short, gout, feat, wback, wfwd):
    for r in range(FROWS):
        for s in range(PEERS):
            at = r * CHAN + s * OWN
            feat[at : at + OWN, :] = block[s, r * OWN : (r + 1) * OWN, :]
    rest = block[:, FEAT:, :].astype(f32)
    for i in range(GHALF):
        piece = rest[:, i * HALF : (i + 1) * HALF, :].reshape(FILT, W)
        gout[i * FILT : (i + 1) * FILT, :] = piece.astype(bf16)
    for p in range(3):
        for q in range(3):
            at = GOUT + (3 * p + q) * HALF
            piece = rest[:, at : at + HALF, :].reshape(FILT, W).astype(bf16)
            wfwd[q * FILT : (q + 1) * FILT, p * W : (p + 1) * W] = piece
            wback[(2 - p) * FILT : (3 - p) * FILT, q * W : (q + 1) * W] = piece
    for r in range(GROWS):
        y = jnp.dot(
            wfwd[...], feat[r * CHAN : (r + 3) * CHAN, :], preferred_element_type=f32
        )
        y = from_left(y[:FILT]) + y[FILT : 2 * FILT] + from_right(y[2 * FILT :])
        part[r * FILT : (r + 1) * FILT, :] = y
        short[r * FILT : (r + 1) * FILT, :] = y.astype(bf16)


def backward(mine, other, g_mine, g_other, feat, wback, out, gout, grad, rows, acc):
    core = lax.rem(lax.axis_index("chan"), NC)
    n = GHALF * FILT
    gout[pl.ds(pl.multiple_of(core * n, FILT), n), :] = g_mine[...]
    gout[pl.ds(pl.multiple_of((1 - core) * n, FILT), n), :] = g_other[...]
    for r in range(GROWS):
        at = slice(r * FILT, (r + 1) * FILT)
        pre = mine[at, :] + other[at, :].astype(f32)
        s = jax.nn.sigmoid(pre)
        rows[at, :] = pre * s
        g = gout[at, :].astype(f32) * s * (1.0 + pre * (1.0 - s))
        grad[at, :] = g.astype(bf16)
    n = ROWS // NC
    kept = rows[pl.ds(pl.multiple_of((1 + core * n) * FILT, FILT), n * FILT), :]
    kept = kept.reshape(n, PEERS, HALF, W)
    for i in range(n):
        acc[:, i * HALF : (i + 1) * HALF, :] = kept[i]

    for r in range(ROWS):
        y = lax.dot_general(
            wback[...],
            grad[r * FILT : (r + 3) * FILT, :],
            (((0,), (0,)), ((), ())),
            preferred_element_type=f32,
        )
        g = from_right(y[:CHAN]) + y[CHAN : 2 * CHAN] + from_left(y[2 * CHAN :])
        out[:, r * OWN : (r + 1) * OWN, :] = g.astype(bf16).reshape(PEERS, OWN, W)

    g = grad[FILT : (ROWS + 1) * FILT, :].astype(f32)
    sides = []
    for moved in (from_right(g), g, from_left(g)):
        m = moved.astype(bf16)
        sides.append(
            jnp.concatenate([m[r * FILT : (r + 1) * FILT] for r in range(ROWS)], 1)
        )
    sides = jnp.concatenate(sides, 0)
    for p in range(3):
        f = jnp.concatenate(
            [feat[(r + p + 1) * CHAN : (r + p + 2) * CHAN, :] for r in range(ROWS)], 1
        )
        d = lax.dot_general(
            sides, f, (((1,), (1,)), ((), ())), preferred_element_type=f32
        )
        for q in range(3):
            at = ACT + (3 * p + q) * HALF
            acc[:, at : at + HALF, :] = d[q * FILT : (q + 1) * FILT].reshape(
                PEERS, HALF, W
            )
    out[:, GRAD:, :] = acc[...].astype(bf16)


def weight_pieces(block, out):
    lane = lax.broadcasted_iota(jnp.int32, (1, 128), 1)
    spaces = NY * NH
    turned = []
    for c in range(NC):
        totals = []
        for z in range(NZ):
            total = 0.0
            for x in range(NX):
                t = (z * NX + x) * NC + c
                total = total + block[t, GRAD:, :].astype(f32)[ACT:]
            totals.append(total)
        for half in range(2):
            at = slice(half * 128, (half + 1) * 128)
            turned.append(
                [
                    [t[:, at] if k == 0 else pltpu.roll(t[:, at], 32 * k, 1) for k in range(4)]
                    for t in totals
                ]
            )
    for s in range(spaces):
        rows = []
        for i in range(PIECE // 8):
            row = jnp.zeros((8, 128), f32)
            for g in range(4):
                tap, z = divmod(4 * i + g, 2)
                if tap < TAPS:
                    part = turned[s // 4][z][(g - s) % 4][tap * 8 : tap * 8 + 8]
                    row = jnp.where(lane // 32 == g, part, row)
            rows.append(row)
        out[s] = jnp.concatenate(rows, 0).astype(bf16)


def finish(
    factor, block, pieces, act_h, up_h, skip_h, out_h, act, grad_up, grad_skip, out, sems
):
    swap = picks(OWN * OWN, OWN * OWN, swapped)
    for c, ref in enumerate((grad_up, grad_skip)):
        rows = []
        for x in range(NX):
            t = x * NC + c
            rows.append(
                block[t, :GRAD, :].astype(f32)
                + block[t + NX * NC, :GRAD, :].astype(f32)
            )
        ref[...] = move(swap, jnp.concatenate(rows, 0).astype(bf16))
    a = block[:, GRAD : GRAD + ACT, :].reshape(PEERS * ACT, W)
    act[...] = move(picks(OWN * OWN, OWN * OWN, act_source), a)

    outs = ((grad_up, up_h), (grad_skip, skip_h), (act, act_h), (out, out_h))
    copies = [
        pltpu.make_async_copy(src, dst, sems.at[i]) for i, (src, dst) in enumerate(outs)
    ]
    for copy in copies[:3]:
        copy.start()

    t = pieces[0].astype(f32)
    for s in range(1, NY * NH):
        t = t + pieces[s].astype(f32)
    t = t * factor
    for g in range(4):
        part = (t if g == 0 else pltpu.roll(t, 128 - 32 * g, 1))[:, :32]
        for i in range(PIECE // 8):
            k = 4 * i + g
            if k < GROUPS:
                out[k * 8 : k * 8 + 8, :] = part[i * 8 : i * 8 + 8]
    copies[3].start()
    for copy in copies:
        copy.wait()


def shards(upsampled, skip_features, conv_weight, grad_output):
    tiles = lax.axis_size("space")
    width = grad_output.shape[3]
    factor = 1.0 / math.sqrt(grad_output.shape[1] * grad_output.shape[2] * tiles * width)

    def turn(partner):
        pairs = []
        for c in range(PEERS):
            for s in range(tiles):
                p = partner(s)
                to = (c, p) if p is not None else (c ^ 1, s)
                pairs.append((c * tiles + s, to[0] * tiles + to[1]))
        return pairs

    def middle_pairs(s):
        p = s + 1 if s % 2 else s - 1
        return p if 0 <= p < tiles else None

    n = OWN * OWN
    anywhere = pl.BlockSpec(memory_space=pltpu.HBM)
    raw = [
        pltpu.with_memory_space_constraint(x, pltpu.HBM)
        for x in (
            upsampled.reshape(n, W),
            skip_features.reshape(n, W),
            grad_output.reshape(n, W),
            conv_weight.transpose(1, 0, 2).reshape(TAPS * OWN, 2 * W),
        )
    ]
    last, first = call(
        edges,
        [pltpu.VMEM((EDGE, W), bf16)] * 2,
        [((n, W), bf16)] * 3 + [pltpu.SemaphoreType.DMA((3, PARTS))],
        in_specs=[anywhere] * 3,
    )(*raw[:3])
    both = ("chan", "space")
    halos = (
        lax.ppermute(last, both, turn(middle_pairs)),
        lax.ppermute(first, "space", [(i, i ^ 1) for i in range(tiles)]),
    )
    held = call(
        by_row,
        [((n, W), bf16)] * 3 + [((TAPS * OWN, 2 * W), bf16)],
        [((n, W), bf16)] * 2 + [pltpu.SemaphoreType.DMA((3, PARTS)), pltpu.SemaphoreType.DMA],
        in_specs=[anywhere] * 4,
    )(*raw)
    (sent,) = call(pack, [((PEERS, IN_BLOCK, W), bf16)])(*held, *halos)
    block = lax.all_to_all(sent, "chan", 0, 0, tiled=True)
    part, short, gout, feat, wback = call(
        forward,
        [
            ((GROWS * FILT, W), f32),
            ((GROWS * FILT, W), bf16),
            ((GHALF * FILT, W), bf16),
            ((FROWS * CHAN, W), bf16),
            ((3 * FILT, 3 * W), bf16),
        ],
        [((3 * FILT, 3 * W), bf16)],
    )(block)
    pair = [(i, i ^ 1) for i in range(PEERS)]
    (sent,) = call(
        backward,
        [((PEERS, OUT_BLOCK, W), bf16)],
        [
            ((GROWS * FILT, W), bf16),
            ((GROWS * FILT, W), bf16),
            ((GROWS * FILT, W), f32),
            ((PEERS, OUT_BLOCK - GRAD, W), f32),
        ],
    )(
        part,
        lax.ppermute(short, "chan", pair),
        gout,
        lax.ppermute(gout, "chan", pair),
        feat,
        wback,
    )
    block = lax.all_to_all(sent, "chan", 0, 0, tiled=True)

    (pieces,) = call(weight_pieces, [((tiles, PIECE, 128), bf16)])(block)
    pieces = lax.all_to_all(pieces, "space", 0, 0, tiled=True)
    activation, grad_up, grad_skip, wgrad = call(
        functools.partial(finish, factor),
        [pltpu.HBM((n, W), bf16)] * 3 + [pltpu.HBM((TAPS * OWN, 32), f32)],
        [((n, W), bf16)] * 3 + [((TAPS * OWN, 32), f32), pltpu.SemaphoreType.DMA((4,))],
        out_specs=[anywhere] * 4,
    )(block, pieces)
    shape = upsampled.shape
    return (
        activation.reshape(shape),
        grad_up.reshape(shape),
        grad_skip.reshape(shape),
        wgrad.reshape(TAPS, OWN, 32).transpose(1, 0, 2),
    )


def solution(mesh):
    tile = P("chan", None, "space", None)
    in_specs = (tile, tile, P("chan", None, None), tile)
    out_specs = (tile, tile, tile, P("chan", None, "space"))
    return jax.shard_map(
        shards, mesh=mesh, in_specs=in_specs, out_specs=out_specs, check_vma=False
    )
```

```python
import functools
import math

import jax
import jax.numpy as jnp
from jax import lax
from jax.experimental import pallas as pl
from jax.experimental.pallas import tpu as pltpu
from jax.sharding import PartitionSpec as P

NZ, NX, NC = 2, 4, 2
PEERS = NZ * NX * NC
NY, NH = 4, 4
W = 256
OWN = 16
HALF = OWN // NZ
ROWS = OWN // NX
FILT = PEERS * HALF
CHAN = PEERS * OWN
TAPS = 9

FROWS = ROWS + 4
GROWS = ROWS + 2
FEAT = FROWS * OWN
GHALF = GROWS // NC
GOUT = GHALF * HALF
IN_BLOCK = FEAT + GOUT + TAPS * HALF
EDGE = 2 * 2 * OWN + OWN
GRAD = ROWS * OWN
ACT = (ROWS // NC) * HALF
OUT_BLOCK = GRAD + ACT + TAPS * HALF
GROUPS = TAPS * OWN // 8
PIECE = -(-GROUPS // 4) * 8

bf16 = jnp.bfloat16
f32 = jnp.float32


def call(body, outs, scratch=(), vmem=32, **specs):
    return pl.pallas_call(
        body,
        out_shape=[jax.ShapeDtypeStruct(*s) if isinstance(s, tuple) else s for s in outs],
        scratch_shapes=[pltpu.VMEM(*s) if isinstance(s, tuple) else s for s in scratch],
        compiler_params=pltpu.CompilerParams(vmem_limit_bytes=vmem * 1024 * 1024),
        **specs,
    )


def picks(rows, cols, source):
    d = lax.broadcasted_iota(jnp.int32, (rows, cols), 0)
    s = lax.broadcasted_iota(jnp.int32, (rows, cols), 1)
    return jnp.where(source(d) == s, 1.0, 0.0).astype(bf16)


def move(matrix, x):
    return jnp.dot(matrix, x, preferred_element_type=f32).astype(bf16)


def swapped(d):
    return ((d & 15) << 4) | (d >> 4)


def gout_source(d):
    f8, core, x, z, i = d & 7, (d >> 3) & 1, (d >> 4) & 3, (d >> 6) & 1, d >> 7
    r = (x << 2) - 1 + core * GHALF + i
    f = (z << 3) | f8
    inside = (f << 4) + r
    return jnp.where(r < 0, 256 + f, jnp.where(r > 15, 272 + f, inside))


def act_source(d):
    f, r = d >> 4, d & 15
    return ((f >> 3) << 7) | (r << 3) | (f & 7)


def fetch(srcs, dsts, sems):
    copies = [
        pltpu.make_async_copy(src, dst, sems.at[i])
        for i, (src, dst) in enumerate(zip(srcs, dsts))
    ]
    for copy in copies:
        copy.start()
    return copies


def edges(up, skip, gout, two, one, u, k, g, sems):
    copies = fetch((up, skip, gout), (u, k, g), sems)
    odd = lax.rem(lax.axis_index("space"), 2) == 1
    n = 2 * OWN
    top = swapped
    bottom = lambda d: swapped(d + OWN * OWN - n)
    near = picks(n, OWN * OWN, lambda d: jnp.where(odd, top(d), bottom(d)))
    far = picks(n, OWN * OWN, lambda d: jnp.where(odd, bottom(d), top(d)))
    near_g = picks(OWN, OWN * OWN, lambda d: (d << 4) + jnp.where(odd, 0, OWN - 1))
    far_g = picks(OWN, OWN * OWN, lambda d: (d << 4) + jnp.where(odd, OWN - 1, 0))
    for i, ref in enumerate((u, k)):
        copies[i].wait()
        x = ref[...]
        one[i * n : (i + 1) * n, :] = move(near, x)
        two[i * n : (i + 1) * n, :] = move(far, x)
    copies[2].wait()
    x = g[...]
    one[2 * n :, :] = move(near_g, x)
    two[2 * n :, :] = move(far_g, x)


def by_row(up, skip, gout, w, up_rows, skip_rows, g_out, w_out, u, k, sems):
    copies = fetch((up, skip, gout, w), (u, k, g_out, w_out), sems)
    swap = picks(OWN * OWN, OWN * OWN, swapped)
    for copy, ref, rows in zip(copies, (u, k), (up_rows, skip_rows)):
        copy.wait()
        rows[...] = move(swap, ref[...])
    for copy in copies[2:]:
        copy.wait()


def pack(up_rows, skip_rows, gout, w, two, one, out):
    n = 2 * OWN
    s = lax.axis_index("space")
    odd = lax.rem(s, 2) == 1
    near = one[...].astype(f32)
    far = jnp.where((s > 0) & (s < NY * NH - 1), two[...].astype(f32), 0.0)
    before = jnp.where(odd, near, far).astype(bf16)
    after = jnp.where(odd, far, near).astype(bf16)
    rows = [
        jnp.concatenate(
            [before[i * n : (i + 1) * n, :], ref[...], after[i * n : (i + 1) * n, :]], 0
        )
        for i, ref in enumerate((up_rows, skip_rows))
    ]
    g = jnp.concatenate([gout[...], before[2 * n :, :], after[2 * n :, :]], 0)
    g = jnp.dot(
        picks(GHALF * PEERS * HALF, OWN * OWN + 2 * OWN, gout_source),
        g,
        preferred_element_type=f32,
    )
    wt = w[...].astype(f32)
    for z in range(NZ):
        for x in range(NX):
            for c in range(NC):
                t = (z * NX + x) * NC + c
                out[t, 0:FEAT, :] = rows[c][x * ROWS * OWN : x * ROWS * OWN + FEAT, :]
                parts = [
                    g[(i * PEERS + t) * HALF : (i * PEERS + t + 1) * HALF]
                    for i in range(GHALF)
                ] + [
                    wt[
                        k * OWN + z * HALF : k * OWN + (z + 1) * HALF,
                        c * W : (c + 1) * W,
                    ]
                    for k in range(TAPS)
                ]
                out[t, FEAT:, :] = jnp.concatenate(parts, 0).astype(bf16)


def column(n=W):
    return lax.broadcasted_iota(jnp.int32, (1, n), 1)


def from_left(x):
    return jnp.where(column() == 0, 0.0, pltpu.roll(x, 1, 1))


def from_right(x):
    return jnp.where(column() == W - 1, 0.0, pltpu.roll(x, W - 1, 1))


def forward(block, part, short, gout, feat, wback, wfwd):
    for r in range(FROWS):
        for s in range(PEERS):
            at = r * CHAN + s * OWN
            feat[at : at + OWN, :] = block[s, r * OWN : (r + 1) * OWN, :]
    rest = block[:, FEAT:, :].astype(f32)
    for i in range(GHALF):
        piece = rest[:, i * HALF : (i + 1) * HALF, :].reshape(FILT, W)
        gout[i * FILT : (i + 1) * FILT, :] = piece.astype(bf16)
    for p in range(3):
        for q in range(3):
            at = GOUT + (3 * p + q) * HALF
            piece = rest[:, at : at + HALF, :].reshape(FILT, W).astype(bf16)
            wfwd[q * FILT : (q + 1) * FILT, p * W : (p + 1) * W] = piece
            wback[(2 - p) * FILT : (3 - p) * FILT, q * W : (q + 1) * W] = piece
    for r in range(GROWS):
        y = jnp.dot(
            wfwd[...], feat[r * CHAN : (r + 3) * CHAN, :], preferred_element_type=f32
        )
        y = from_left(y[:FILT]) + y[FILT : 2 * FILT] + from_right(y[2 * FILT :])
        part[r * FILT : (r + 1) * FILT, :] = y
        short[r * FILT : (r + 1) * FILT, :] = y.astype(bf16)


def backward(mine, other, g_mine, g_other, feat, wback, out, gout, grad, rows, acc):
    core = lax.rem(lax.axis_index("chan"), NC)
    n = GHALF * FILT
    gout[pl.ds(pl.multiple_of(core * n, FILT), n), :] = g_mine[...]
    gout[pl.ds(pl.multiple_of((1 - core) * n, FILT), n), :] = g_other[...]
    for r in range(GROWS):
        at = slice(r * FILT, (r + 1) * FILT)
        pre = mine[at, :] + other[at, :].astype(f32)
        s = jax.nn.sigmoid(pre)
        rows[at, :] = pre * s
        g = gout[at, :].astype(f32) * s * (1.0 + pre * (1.0 - s))
        grad[at, :] = g.astype(bf16)
    n = ROWS // NC
    kept = rows[pl.ds(pl.multiple_of((1 + core * n) * FILT, FILT), n * FILT), :]
    kept = kept.reshape(n, PEERS, HALF, W)
    for i in range(n):
        acc[:, i * HALF : (i + 1) * HALF, :] = kept[i]

    for r in range(ROWS):
        y = lax.dot_general(
            wback[...],
            grad[r * FILT : (r + 3) * FILT, :],
            (((0,), (0,)), ((), ())),
            preferred_element_type=f32,
        )
        g = from_right(y[:CHAN]) + y[CHAN : 2 * CHAN] + from_left(y[2 * CHAN :])
        out[:, r * OWN : (r + 1) * OWN, :] = g.astype(bf16).reshape(PEERS, OWN, W)

    g = grad[FILT : (ROWS + 1) * FILT, :].astype(f32)
    sides = []
    for moved in (from_right(g), g, from_left(g)):
        m = moved.astype(bf16)
        sides.append(
            jnp.concatenate([m[r * FILT : (r + 1) * FILT] for r in range(ROWS)], 1)
        )
    sides = jnp.concatenate(sides, 0)
    for p in range(3):
        f = jnp.concatenate(
            [feat[(r + p + 1) * CHAN : (r + p + 2) * CHAN, :] for r in range(ROWS)], 1
        )
        d = lax.dot_general(
            sides, f, (((1,), (1,)), ((), ())), preferred_element_type=f32
        )
        for q in range(3):
            at = ACT + (3 * p + q) * HALF
            acc[:, at : at + HALF, :] = d[q * FILT : (q + 1) * FILT].reshape(
                PEERS, HALF, W
            )
    out[:, GRAD:, :] = acc[...].astype(bf16)


def weight_pieces(block, out):
    lane = lax.broadcasted_iota(jnp.int32, (1, 128), 1)
    spaces = NY * NH
    turned = []
    for c in range(NC):
        totals = []
        for z in range(NZ):
            total = 0.0
            for x in range(NX):
                t = (z * NX + x) * NC + c
                total = total + block[t, GRAD:, :].astype(f32)[ACT:]
            totals.append(total)
        for half in range(2):
            at = slice(half * 128, (half + 1) * 128)
            turned.append(
                [
                    [t[:, at] if k == 0 else pltpu.roll(t[:, at], 32 * k, 1) for k in range(4)]
                    for t in totals
                ]
            )
    for s in range(spaces):
        rows = []
        for i in range(PIECE // 8):
            row = jnp.zeros((8, 128), f32)
            for g in range(4):
                tap, z = divmod(4 * i + g, 2)
                if tap < TAPS:
                    part = turned[s // 4][z][(g - s) % 4][tap * 8 : tap * 8 + 8]
                    row = jnp.where(lane // 32 == g, part, row)
            rows.append(row)
        out[s] = jnp.concatenate(rows, 0).astype(bf16)


def finish(
    factor, block, pieces, act_h, up_h, skip_h, out_h, act, grad_up, grad_skip, out, sems
):
    swap = picks(OWN * OWN, OWN * OWN, swapped)
    for c, ref in enumerate((grad_up, grad_skip)):
        rows = []
        for x in range(NX):
            t = x * NC + c
            rows.append(
                block[t, :GRAD, :].astype(f32)
                + block[t + NX * NC, :GRAD, :].astype(f32)
            )
        ref[...] = move(swap, jnp.concatenate(rows, 0).astype(bf16))
    a = block[:, GRAD : GRAD + ACT, :].reshape(PEERS * ACT, W)
    act[...] = move(picks(OWN * OWN, OWN * OWN, act_source), a)

    outs = ((grad_up, up_h), (grad_skip, skip_h), (act, act_h), (out, out_h))
    copies = [
        pltpu.make_async_copy(src, dst, sems.at[i]) for i, (src, dst) in enumerate(outs)
    ]
    for copy in copies[:3]:
        copy.start()

    t = pieces[0].astype(f32)
    for s in range(1, NY * NH):
        t = t + pieces[s].astype(f32)
    t = t * factor
    for g in range(4):
        part = (t if g == 0 else pltpu.roll(t, 128 - 32 * g, 1))[:, :32]
        for i in range(PIECE // 8):
            k = 4 * i + g
            if k < GROUPS:
                out[k * 8 : k * 8 + 8, :] = part[i * 8 : i * 8 + 8]
    copies[3].start()
    for copy in copies:
        copy.wait()


def shards(upsampled, skip_features, conv_weight, grad_output):
    tiles = lax.axis_size("space")
    width = grad_output.shape[3]
    factor = 1.0 / math.sqrt(grad_output.shape[1] * grad_output.shape[2] * tiles * width)

    def turn(partner):
        pairs = []
        for c in range(PEERS):
            for s in range(tiles):
                p = partner(s)
                to = (c, p) if p is not None else (c ^ 1, s)
                pairs.append((c * tiles + s, to[0] * tiles + to[1]))
        return pairs

    def middle_pairs(s):
        p = s + 1 if s % 2 else s - 1
        return p if 0 <= p < tiles else None

    n = OWN * OWN
    anywhere = pl.BlockSpec(memory_space=pltpu.HBM)
    raw = [
        pltpu.with_memory_space_constraint(x, pltpu.HBM)
        for x in (
            upsampled.reshape(n, W),
            skip_features.reshape(n, W),
            grad_output.reshape(n, W),
            conv_weight.transpose(1, 0, 2).reshape(TAPS * OWN, 2 * W),
        )
    ]
    last, first = call(
        edges,
        [pltpu.VMEM((EDGE, W), bf16)] * 2,
        [((n, W), bf16)] * 3 + [pltpu.SemaphoreType.DMA((3,))],
        in_specs=[anywhere] * 3,
    )(*raw[:3])
    both = ("chan", "space")
    halos = (
        lax.ppermute(last, both, turn(middle_pairs)),
        lax.ppermute(first, "space", [(i, i ^ 1) for i in range(tiles)]),
    )
    held = call(
        by_row,
        [((n, W), bf16)] * 3 + [((TAPS * OWN, 2 * W), bf16)],
        [((n, W), bf16)] * 2 + [pltpu.SemaphoreType.DMA((4,))],
        in_specs=[anywhere] * 4,
    )(*raw)
    (sent,) = call(pack, [((PEERS, IN_BLOCK, W), bf16)])(*held, *halos)
    block = lax.all_to_all(sent, "chan", 0, 0, tiled=True)
    part, short, gout, feat, wback = call(
        forward,
        [
            ((GROWS * FILT, W), f32),
            ((GROWS * FILT, W), bf16),
            ((GHALF * FILT, W), bf16),
            ((FROWS * CHAN, W), bf16),
            ((3 * FILT, 3 * W), bf16),
        ],
        [((3 * FILT, 3 * W), bf16)],
    )(block)
    pair = [(i, i ^ 1) for i in range(PEERS)]
    (sent,) = call(
        backward,
        [((PEERS, OUT_BLOCK, W), bf16)],
        [
            ((GROWS * FILT, W), bf16),
            ((GROWS * FILT, W), bf16),
            ((GROWS * FILT, W), f32),
            ((PEERS, OUT_BLOCK - GRAD, W), f32),
        ],
    )(
        part,
        lax.ppermute(short, "chan", pair),
        gout,
        lax.ppermute(gout, "chan", pair),
        feat,
        wback,
    )
    block = lax.all_to_all(sent, "chan", 0, 0, tiled=True)

    (pieces,) = call(weight_pieces, [((tiles, PIECE, 128), bf16)])(block)
    pieces = lax.all_to_all(pieces, "space", 0, 0, tiled=True)
    activation, grad_up, grad_skip, wgrad = call(
        functools.partial(finish, factor),
        [pltpu.HBM((n, W), bf16)] * 3 + [pltpu.HBM((TAPS * OWN, 32), f32)],
        [((n, W), bf16)] * 3 + [((TAPS * OWN, 32), f32), pltpu.SemaphoreType.DMA((4,))],
        out_specs=[anywhere] * 4,
    )(block, pieces)
    shape = upsampled.shape
    return (
        activation.reshape(shape),
        grad_up.reshape(shape),
        grad_skip.reshape(shape),
        wgrad.reshape(TAPS, OWN, 32).transpose(1, 0, 2),
    )


def solution(mesh):
    tile = P("chan", None, "space", None)
    in_specs = (tile, tile, P("chan", None, None), tile)
    out_specs = (tile, tile, tile, P("chan", None, "space"))
    return jax.shard_map(
        shards, mesh=mesh, in_specs=in_specs, out_specs=out_specs, check_vma=False
    )
```
